32 devices in a mesh: sec: 4 (over y, core), dom: 8 (over z, x).
Axes of the slice: x: 2, y: 2, z: 4, core: 2. Of those that a mesh axis runs over, the one named last changes fastest.
Arguments:
- flow_state: bfloat16 [270, 32768], P(None, ('sec', 'dom')), may hold values from -6 to 6
- base_geometry: float32 [4, 32768], P(None, ('sec', 'dom')), may hold values from 0.5 to 2
- anchor_weight: float32 [32768], P(('sec', 'dom')), may hold values from 0 to 1.5
- wall_anchor: int32 [32768], P(('sec', 'dom')), may hold values from 0 to 32767
- face_nbr: int32 [6, 32768], P(None, ('sec', 'dom')), may hold values from 0 to 1151, as said below
- volume_ops: bfloat16 [4, 270, 270], replicated, may hold values from -0.375 to 0.375
- lift_ops: bfloat16 [6, 270, 90], replicated, may hold values from -0.625 to 0.625
- face_jac: bfloat16 [6, 2, 5, 5], replicated, may hold values from -2.5 to 2.5
- wall_load: float32 [3, 256, 128], P(None, ('sec', 'dom')), may hold values from -6 to 6
- wall_stiff: float32 [3, 256, 128], P(None, ('sec', 'dom')), may hold values from 0.01 to 0.3
Outputs:
- flow_residual: bfloat16 [270, 32768], P(None, ('sec', 'dom'))
- wall_disp: float32 [3, 256, 128], P(None, ('sec', 'dom'))
The draws below stay inside these ranges and needn't reach their ends.
Inputs may be any that keep to these rules, and one draw needn't show every extreme that they name: `face_nbr`: for faces 0 to 3 a value v >= 1024 names element v - 1024 (below 128) of the device one step lower (faces 0 and 2) or higher (faces 1 and 3), cyclically, along dom (faces 0 and 1) or sec (faces 2 and 3); a smaller value names an element of the element's own device. Faces 4 and 5 always name an element of the own device.
All inputs are finite; a program needn't handle non-finite values.
Results may differ from the reference program's by a relative error of at most 0.0046.
Values may be sent and summed in bfloat16 or wider, within the bound.
No kernel may reach another device: no remote copies, remote signals or barrier semaphores. Data moves between devices by JAX's collectives and lax.ppermute only.
A program may use at most 320 MiB of HBM per device.

```python
import math
import jax
import jax.numpy as jnp
from jax import lax

NV = 5
NQ = 270
NF = 90
E_DEV = 1024
HB = 128
NE = 32768
WB = 128
WA = 256
NW = 32768
ITERS = 8
N_SEC = 4
N_DOM = 8


def draw_face_nbr(key, part):
    first = jax.random.fold_in(key, 11)
    second = jax.random.fold_in(key, 12)
    third = jax.random.fold_in(key, 13)
    local_pick = jax.random.randint(first, (6, NE), 0, E_DEV, dtype=jnp.int32)
    remote_pick = jax.random.randint(second, (6, NE), 0, HB, dtype=jnp.int32) + E_DEV
    remote_flag = jax.random.randint(third, (6, NE), 0, 2, dtype=jnp.int32) == 1
    crossing = jnp.arange(6, dtype=jnp.int32)[:, None] < 4
    neighbours = jnp.where(remote_flag & crossing, remote_pick, local_pick)
    neighbours = neighbours.at[0, 0].set(E_DEV + HB - 1)
    neighbours = neighbours.at[4, 0].set(0)
    return neighbours.astype(jnp.int32)


def plant(result, rng, least, top_value):
    extent = result.shape
    place = [jax.random.randint(jax.random.fold_in(rng, axis), (), 0, extent[axis]) for axis in range(len(extent))]
    result = result.at[tuple(place)].set(least)
    longest = extent.index(max(extent))
    place[longest] = (place[longest] + 1) % extent[longest]
    return result.at[tuple(place)].set(top_value)


def levels(rng, shape, split, smallest, largest):
    factor_of, own = 1.0, jax.random.fold_in(rng, 6)
    for position, blocks in split:
        draws = jnp.exp(jax.random.uniform(jax.random.fold_in(own, position), (blocks,), jnp.float32, smallest / len(split), largest / len(split)))
        factor_of = factor_of * jnp.repeat(draws, shape[position] // blocks).reshape([-1 if axis == position else 1 for axis in range(len(shape))])
    return factor_of


def centred(key, shape, spread, reach, split=(), kind=jnp.bfloat16):
    drawn = jax.random.normal(key, shape, jnp.float32) * spread
    if len(split) > 0:
        drawn = levels(key, shape, split, -0.22, 0.18) * drawn
    return jnp.clip(drawn, min=-reach, max=reach).astype(kind)


def setup_inputs(seed: int = 0) -> dict:
    seeds = jax.random.split(jax.random.key(seed), 11)
    flow_state = centred(seeds[0], (NQ, NE), 1.0, 6.0, ((1, 32),))
    base_geometry = jnp.clip(jnp.exp(math.log(2.0) - 1.3862944 * jax.random.uniform(seeds[1], (4, NE), jnp.float32) ** levels(seeds[1], (4, NE), ((1, 32),), -0.2, 0.2)), 0.5, 2.0)
    anchor_weight = jnp.clip(1.5 * jax.random.uniform(seeds[2], (NE,), jnp.float32) ** levels(seeds[2], (NE,), ((0, 32),), -0.2, 0.2), 0.0, 1.5)
    wall_anchor = plant(jax.random.randint(seeds[3], (NE,), 0, NW), jax.random.fold_in(seeds[3], 1), 0, NW - 1).astype(jnp.int32)
    face_nbr = draw_face_nbr(jax.random.fold_in(seeds[10], 71), 0)
    volume_ops = centred(seeds[5], (4, NQ, NQ), NQ ** -0.5, 0.375)
    lift_ops = centred(seeds[6], (6, NQ, NF), NF ** -0.5, 0.625)
    face_jac = centred(seeds[7], (6, 2, NV, NV), NV ** -0.5, 2.5)
    wall_load = centred(seeds[8], (3, WA, WB), 1.0, 6.0, ((1, 32),), jnp.float32)
    wall_stiff = jnp.clip(jnp.exp(math.log(0.3) - 3.4011974 * jax.random.uniform(seeds[9], (3, WA, WB), jnp.float32) ** levels(seeds[9], (3, WA, WB), ((1, 32),), -0.2, 0.2)), 0.01, 0.3)
    return dict(flow_state=flow_state, base_geometry=base_geometry, anchor_weight=anchor_weight, wall_anchor=wall_anchor, face_nbr=face_nbr, volume_ops=volume_ops, lift_ops=lift_ops, face_jac=face_jac, wall_load=wall_load, wall_stiff=wall_stiff)


def wall_operator(field, stiffness):
    padded = jnp.pad(field, ((0, 0), (1, 1), (1, 1)))
    beside = padded[:, 2:, 1:-1] + padded[:, :-2, 1:-1] + padded[:, 1:-1, 2:] + padded[:, 1:-1, :-2]
    return (4.0 + stiffness) * field - beside


def face_trace(values, face):
    shaped = values.reshape(NV, 2, 3, 3, 3, values.shape[1])
    picked = lax.index_in_dim(shaped, 0 if face % 2 == 0 else 2, 2 + face // 2, keepdims=False)
    return picked.reshape(NV * 18, values.shape[1])


def residual_block(state, geometry, neighbours, remotes, volume_ops, lift_ops, face_jac):
    summed = jnp.zeros(state.shape, jnp.float32)
    for direction in range(4):
        summed = summed + geometry[direction][None, :] * jnp.dot(volume_ops[direction], state, preferred_element_type=jnp.float32)
    identity = jnp.eye(18, dtype=jnp.bfloat16)
    for face in range(6):
        own_trace = face_trace(state, face)
        opposite = face_trace(state, face ^ 1)
        if face < 4:
            candidates = jnp.concatenate([opposite, remotes[face]], axis=1)
        else:
            candidates = opposite
        neighbour_trace = jnp.take(candidates, neighbours[face], axis=1)
        own_jac = jnp.kron(face_jac[face, 0], identity)
        other_jac = jnp.kron(face_jac[face, 1], identity)
        face_flux = geometry[face // 2][None, :] * (jnp.dot(own_jac, own_trace, preferred_element_type=jnp.float32) + jnp.dot(other_jac, neighbour_trace, preferred_element_type=jnp.float32))
        face_flux = face_flux.astype(jnp.bfloat16)
        summed = summed + jnp.dot(lift_ops[face], face_flux, preferred_element_type=jnp.float32)
    return summed.astype(jnp.bfloat16)


def reference(flow_state, base_geometry, anchor_weight, wall_anchor, face_nbr, volume_ops, lift_ops, face_jac, wall_load, wall_stiff):
    wall_disp = jnp.zeros_like(wall_load)
    resid = wall_load
    search = wall_load
    norm_now = jnp.sum(resid * resid)
    for iteration in range(ITERS):
        image = wall_operator(search, wall_stiff)
        step_size = norm_now / jnp.sum(search * image)
        wall_disp = wall_disp + step_size * search
        resid = resid - step_size * image
        norm_next = jnp.sum(resid * resid)
        search = resid + (norm_next / norm_now) * search
        norm_now = norm_next
    flattened = wall_disp.reshape(3, WA * WB)
    disp_at = jnp.take(flattened, wall_anchor, axis=1)
    geometry = jnp.concatenate([base_geometry[:3] * jnp.exp(anchor_weight[None, :] * disp_at), base_geometry[3:]], axis=0)

    def block_of(array, which):
        return lax.dynamic_slice_in_dim(array, (which * E_DEV).astype(jnp.int32), E_DEV, 1)

    def one_device(device):
        sec_pos = device // N_DOM
        dom_pos = device % N_DOM
        dom_low = sec_pos * N_DOM + (dom_pos - 1) % N_DOM
        dom_high = sec_pos * N_DOM + (dom_pos + 1) % N_DOM
        sec_low = ((sec_pos - 1) % N_SEC) * N_DOM + dom_pos
        sec_high = ((sec_pos + 1) % N_SEC) * N_DOM + dom_pos
        remotes = [
            face_trace(block_of(flow_state, dom_low)[:, :HB], 1),
            face_trace(block_of(flow_state, dom_high)[:, :HB], 0),
            face_trace(block_of(flow_state, sec_low)[:, :HB], 3),
            face_trace(block_of(flow_state, sec_high)[:, :HB], 2),
        ]
        return residual_block(block_of(flow_state, device), block_of(geometry, device), block_of(face_nbr, device), remotes, volume_ops, lift_ops, face_jac)

    blocks = lax.map(one_device, jnp.arange(N_SEC * N_DOM, dtype=jnp.int32))
    flow_residual = jnp.moveaxis(blocks, 0, 1).reshape(NQ, NE)
    return flow_residual, wall_disp
```

```python
import functools

import jax
import jax.numpy as jnp
import numpy as np
from jax import lax
from jax.experimental import pallas as pl
from jax.experimental.pallas import tpu as pltpu
from jax.sharding import PartitionSpec as P

NV = 5
ITERS = 8
NODES = 18
SLOT = 96
TILE = 8
WIDE = 256
BOTH = ("sec", "dom")


def face_rows(face):
    rows = np.arange(NV * 54).reshape(NV * 2, 3, 3, 3)
    return np.take(rows, 0 if face % 2 == 0 else 2, axis=1 + face // 2).reshape(-1)


def picker(faces, unknowns):
    picks = np.zeros((len(faces) * SLOT, unknowns), np.float32)
    for slot, face in enumerate(faces):
        rows = face_rows(face)
        picks[slot * SLOT + np.arange(rows.size), rows] = 1
    return jnp.asarray(picks, jnp.bfloat16)


def kron_parts(sides):
    row = np.arange(SLOT)
    valid = row < NV * NODES
    variable, node = row // NODES, row % NODES
    left = np.zeros((SLOT, NV), np.float32)
    left[row[valid], variable[valid]] = 1
    right = np.zeros((sides * NV, sides * SLOT), np.float32)
    for side in range(sides):
        right[side * NV + variable[valid], side * SLOT + row[valid]] = 1
    same = (node[:, None] == node[None, :]) & valid[:, None] & valid[None, :]
    return (
        jnp.asarray(left, jnp.bfloat16),
        jnp.asarray(right, jnp.bfloat16),
        jnp.asarray(np.concatenate([same, same], axis=1), jnp.float32),
    )


def dot(a, b):
    return jnp.dot(a, b, preferred_element_type=jnp.float32)


def head_kernel(state_ref, picks_ref, *out_refs):
    head = state_ref[...]
    for slot, out_ref in enumerate(out_refs):
        out_ref[...] = dot(picks_ref[slot * SLOT : (slot + 1) * SLOT, :], head).astype(jnp.bfloat16)


def head_traces(flow_state, head_count):
    unknowns = flow_state.shape[0]
    faces = (1, 0, 3, 2)
    return pl.pallas_call(
        head_kernel,
        grid=(1,),
        in_specs=[
            pl.BlockSpec((unknowns, head_count), lambda i: (0, 0)),
            pl.BlockSpec((len(faces) * SLOT, unknowns), lambda i: (0, 0)),
        ],
        out_specs=[pl.BlockSpec((SLOT, head_count), lambda i: (0, 0))] * len(faces),
        out_shape=[jax.ShapeDtypeStruct((SLOT, head_count), jnp.bfloat16)] * len(faces),
        name="head_traces",
    )(flow_state, picker(faces, unknowns))


def flow_kernel(
    state_ref, nbr_ref, from0, from1, from2, from3, weights_ref, jac_ref, picks_ref, left_ref, right_ref, same_ref,
    out_ref, trace_ref, flux_mat_ref, gathered_ref,
):
    step = pl.program_id(0)
    chunks = state_ref.shape[1] // WIDE
    remotes = (from0, from1, from2, from3)

    @pl.when(step == 0)
    def _():
        def traces(chunk, carry):
            cols = pl.ds(pl.multiple_of(chunk * WIDE, WIDE), WIDE)
            trace_ref[:, cols] = dot(picks_ref[...], state_ref[:, cols]).astype(jnp.bfloat16)
            return carry

        lax.fori_loop(0, chunks, traces, 0)
        spread = dot(left_ref[...], jac_ref[...]).astype(jnp.bfloat16)
        spread = dot(spread, right_ref[...])
        for face in range(6):
            both = spread[:, face * 2 * SLOT : (face + 1) * 2 * SLOT]
            flux_mat_ref[face] = (both * same_ref[...]).astype(jnp.bfloat16)

    here = pl.ds(pl.multiple_of(step * WIDE, WIDE), WIDE)
    lane = lax.broadcasted_iota(jnp.int32, (WIDE, WIDE), 0)
    fluxes = []
    for face in range(6):
        index = nbr_ref[face : face + 1, :]
        part = index // WIDE
        pick = jnp.where(lane == index - part * WIDE, 1.0, 0.0).astype(jnp.bfloat16)
        opposite = (face ^ 1) * SLOT
        found = jnp.zeros((SLOT, WIDE), jnp.float32)
        for chunk in range(chunks):
            source = trace_ref[opposite : opposite + SLOT, chunk * WIDE : (chunk + 1) * WIDE]
            found = jnp.where(part == chunk, dot(source, pick), found)
        if face < 4:
            source = remotes[face][...]
            found = jnp.where(part == chunks, dot(source, pick[: source.shape[1], :]), found)
        gathered_ref[:SLOT, :] = trace_ref[face * SLOT : (face + 1) * SLOT, here]
        gathered_ref[SLOT:, :] = found.astype(jnp.bfloat16)
        fluxes.append(dot(flux_mat_ref[face], gathered_ref[...]).astype(jnp.bfloat16))
    own = state_ref[:, here]
    for direction in range(4):
        if direction < 3:
            operand = jnp.concatenate([fluxes[2 * direction], fluxes[2 * direction + 1], own], axis=0)
            out_ref[direction] = dot(weights_ref[direction], operand)
        else:
            out_ref[direction] = dot(weights_ref[direction, :, 2 * SLOT :], own)


def flow_parts(flow_state, face_nbr, remotes, weights, jac):
    unknowns, count = flow_state.shape
    head_count = remotes[0].shape[1]
    picks = picker(range(6), unknowns)
    left, right, same = kron_parts(12)

    def whole(array):
        return pl.BlockSpec(array.shape, lambda i: (0,) * array.ndim)

    args = (flow_state, face_nbr, *remotes, weights, jac, picks, left, right, same)
    specs = [whole(a) for a in args]
    specs[1] = pl.BlockSpec((6, WIDE), lambda i: (0, i))
    return pl.pallas_call(
        flow_kernel,
        grid=(count // WIDE,),
        in_specs=specs,
        out_specs=pl.BlockSpec((4, unknowns, WIDE), lambda i: (0, 0, i)),
        out_shape=jax.ShapeDtypeStruct((4, unknowns, count), jnp.float32),
        scratch_shapes=[
            pltpu.VMEM((6 * SLOT, count), jnp.bfloat16),
            pltpu.VMEM((6, SLOT, 2 * SLOT), jnp.bfloat16),
            pltpu.VMEM((2 * SLOT, WIDE), jnp.bfloat16),
        ],
        compiler_params=pltpu.CompilerParams(vmem_limit_bytes=24 << 20),
        cost_estimate=pl.CostEstimate(flops=4 << 30, bytes_accessed=8 << 20, transcendentals=0),
        name="flow_parts",
    )(*args)


def total(tile):
    return jnp.sum(jnp.sum(tile, axis=0, keepdims=True), axis=1, keepdims=True)


def wall_kernel(
    masks, rows, own_rows,
    near_ref, far_ref, base_ref, follow_ref, anchor_ref, parts_hbm, residual_ref, disp_ref,
    disp, resid, search, image, diag, parts_ref, copy_sem,
):
    comps = 3
    tiles = rows // TILE
    me = lax.axis_index(BOTH)
    fetch = pltpu.make_async_copy(parts_hbm, parts_ref, copy_sem)
    fetch.start()

    def strided(block):
        first = block * TILE
        return pl.ds((first % tiles) * TILE + first // tiles, TILE, stride=TILE)

    half = near_ref.shape[0]
    for slot in range(2 * half):
        ref, at = (near_ref, slot) if slot < half else (far_ref, slot - half)
        device = jnp.bitwise_xor(me, masks[slot])
        for block in range(own_rows // TILE):
            to = strided(device * (own_rows // TILE) + block)
            for c in range(comps):
                first = c * own_rows + block * TILE
                resid[c, to, :] = ref[at, first : first + TILE, :]
                first += comps * own_rows
                diag[c, to, :] = 4.0 + ref[at, first : first + TILE, :]

    lane = lax.broadcasted_iota(jnp.int32, (TILE, 128), 1)
    sub = lax.broadcasted_iota(jnp.int32, (TILE, 128), 0)
    group = 32 if tiles % 32 == 0 else 8
    zero = jnp.zeros((TILE, 128), jnp.float32)

    def at(tile):
        return pl.ds(pl.multiple_of(tile * TILE, TILE), TILE)

    def each_tile(body, carry):
        for c in range(comps):
            def some(chunk, carry, c=c):
                for k in range(group):
                    carry = body(c, chunk * group + k, carry)
                return carry

            if tiles == group:
                carry = some(0, carry)
            else:
                carry = lax.fori_loop(0, tiles // group, some, carry)
        return carry

    def load(c, tile, acc):
        value = resid[c, at(tile), :]
        search[c, at(tile + 1), :] = value
        disp[c, at(tile), :] = zero
        return acc + value * value

    norm = total(each_tile(load, zero))

    def iterate(position, norm_now):
        for c in range(comps):
            last = search[c, at(tiles), :]
            search[c, at(0), :] = jnp.where(sub == 0, 0.0, pltpu.roll(last, 1, 0))
            first = search[c, at(1), :]
            search[c, at(tiles + 1), :] = jnp.where(sub == TILE - 1, 0.0, pltpu.roll(first, TILE - 1, 0))

        def apply(c, tile, acc):
            value = search[c, at(tile + 1), :]
            beside = search[c, at(tile), :] + search[c, at(tile + 2), :]
            beside += jnp.where(lane == 0, 0.0, pltpu.roll(value, 1, 1))
            beside += jnp.where(lane == 127, 0.0, pltpu.roll(value, 127, 1))
            result = diag[c, at(tile), :] * value - beside
            image[c, at(tile), :] = result
            return acc + value * result

        step_size = norm_now / total(each_tile(apply, zero))

        def move(c, tile, acc):
            disp[c, at(tile), :] += step_size * search[c, at(tile + 1), :]
            value = resid[c, at(tile), :] - step_size * image[c, at(tile), :]
            resid[c, at(tile), :] = value
            return acc + value * value

        norm_next = total(each_tile(move, zero))
        ratio = norm_next / norm_now

        def turn(c, tile, acc):
            search[c, at(tile + 1), :] = resid[c, at(tile), :] + ratio * search[c, at(tile + 1), :]
            return acc

        each_tile(turn, 0)
        return norm_next

    lax.fori_loop(0, ITERS, iterate, norm)

    for block in range(own_rows // TILE):
        for c in range(comps):
            disp_ref[c, block * TILE : (block + 1) * TILE, :] = disp[c, strided(me * (own_rows // TILE) + block), :]

    anchor = anchor_ref[...]
    count = anchor.shape[1]
    row = anchor // 128
    column = anchor - row * 128
    upper = row // tiles
    place = (row - upper * tiles) * TILE + upper
    pick = jnp.where(lax.broadcasted_iota(jnp.int32, (128, count), 0) == column, 1.0, 0.0).astype(jnp.bfloat16)
    pick = jnp.concatenate([pick, pick], axis=0)
    some_rows = 128
    row_of = lax.broadcasted_iota(jnp.int32, (some_rows, count), 0)

    def look(chunk, sums):
        first = pl.multiple_of(chunk * some_rows, some_rows)
        hit = row_of == place - first
        out = []
        for c in range(comps):
            value = disp[c, pl.ds(first, some_rows), :]
            coarse = value.astype(jnp.bfloat16)
            fine = (value - coarse.astype(jnp.float32)).astype(jnp.bfloat16)
            found = dot(jnp.concatenate([coarse, fine], axis=1), pick)
            found = jnp.where(hit, found, 0.0).reshape(some_rows // TILE, TILE, count)
            out.append(sums[c] + jnp.sum(found, axis=0))
        return tuple(out)

    sums = lax.fori_loop(0, rows // some_rows, look, (jnp.zeros((TILE, count), jnp.float32),) * comps)
    follow = follow_ref[...]
    geometry = [
        base_ref[c : c + 1, :] * jnp.exp(follow * jnp.sum(sums[c], axis=0, keepdims=True)) for c in range(comps)
    ]
    geometry.append(base_ref[comps : comps + 1, :])
    fetch.wait()
    unknowns = residual_ref.shape[0]
    for first in range(0, unknowns, 16):
        some = slice(first, min(first + 16, unknowns))
        value = geometry[0] * parts_ref[0, some, :]
        for direction in range(1, 4):
            value += geometry[direction] * parts_ref[direction, some, :]
        residual_ref[some, :] = value.astype(jnp.bfloat16)


def wall_and_residual(near, far, masks, base_geometry, anchor_weight, wall_anchor, parts, own_rows):
    rows = own_rows * 2 * near.shape[0]
    _, unknowns, count = parts.shape
    field = pltpu.VMEM((3, rows, 128), jnp.float32)
    vmem = pl.BlockSpec(memory_space=pltpu.VMEM)
    return pl.pallas_call(
        functools.partial(wall_kernel, masks, rows, own_rows),
        in_specs=[vmem, vmem, vmem, vmem, vmem, pl.BlockSpec(memory_space=pl.ANY)],
        out_specs=[vmem, vmem],
        out_shape=[
            jax.ShapeDtypeStruct((unknowns, count), jnp.bfloat16),
            jax.ShapeDtypeStruct((3, own_rows, 128), jnp.float32),
        ],
        scratch_shapes=[
            field,
            field,
            pltpu.VMEM((3, rows + 2 * TILE, 128), jnp.float32),
            field,
            field,
            pltpu.VMEM(parts.shape, jnp.float32),
            pltpu.SemaphoreType.DMA,
        ],
        compiler_params=pltpu.CompilerParams(vmem_limit_bytes=(16 << 20) + 16 * rows * 3 * 128 * 4),
        cost_estimate=pl.CostEstimate(flops=1 << 30, bytes_accessed=8 << 20, transcendentals=0),
        name="wall_and_residual",
    )(near, far, base_geometry, anchor_weight[None, :], wall_anchor[None, :], parts)


def shifted(x, axis, by):
    peers = lax.axis_size(axis)
    return lax.ppermute(x, axis, [(i, (i + by) % peers) for i in range(peers)])


def gather_stages(mesh):
    def bits(axis):
        assert mesh.shape[axis] & (mesh.shape[axis] - 1) == 0
        return [(axis, 1 << b) for b in reversed(range(mesh.shape[axis].bit_length() - 1))]

    return bits("dom") + bits("sec")


def on_device(
    stages, n_dom,
    flow_state, base_geometry, anchor_weight, wall_anchor, face_nbr, volume_ops, lift_ops, face_jac, wall_load, wall_stiff,
):
    own_rows, width = wall_load.shape[1:]
    wall = jnp.concatenate([wall_load, wall_stiff], axis=0).reshape(1, 6 * own_rows, width)
    masks = [0]
    far = wall
    for position, (axis, bit) in enumerate(stages):
        if position > 0:
            wall = jnp.concatenate([wall, far], axis=0)
        far = lax.ppermute(wall, axis, [(i, i ^ bit) for i in range(lax.axis_size(axis))])
        masks += [m ^ (bit * n_dom if axis == "sec" else bit) for m in masks]

    head_count = flow_state.shape[1] // 8
    heads = head_traces(flow_state, head_count)
    remotes = [
        shifted(heads[0], "dom", 1),
        shifted(heads[1], "dom", -1),
        shifted(heads[2], "sec", 1),
        shifted(heads[3], "sec", -1),
    ]
    lifts = jnp.pad(lift_ops, ((0, 2), (0, 0), (0, SLOT - lift_ops.shape[2])))
    weights = jnp.concatenate([lifts[0::2], lifts[1::2], volume_ops], axis=2)
    jac = face_jac.transpose(2, 0, 1, 3).reshape(NV, 12 * NV)
    parts = flow_parts(flow_state, face_nbr, remotes, weights, jac)
    return wall_and_residual(wall, far, masks, base_geometry, anchor_weight, wall_anchor, parts, own_rows)


def solution(mesh):
    return jax.shard_map(
        functools.partial(on_device, gather_stages(mesh), mesh.shape["dom"]),
        mesh=mesh,
        in_specs=(
            P(None, BOTH),
            P(None, BOTH),
            P(BOTH),
            P(BOTH),
            P(None, BOTH),
            P(),
            P(),
            P(),
            P(None, BOTH, None),
            P(None, BOTH, None),
        ),
        out_specs=(P(None, BOTH), P(None, BOTH, None)),
        check_vma=False,
    )
```

```python
import functools

import jax
import jax.numpy as jnp
import numpy as np
from jax import lax
from jax.experimental import pallas as pl
from jax.experimental.pallas import tpu as pltpu
from jax.sharding import PartitionSpec as P

NV = 5
ITERS = 8
NODES = 18
SLOT = 96
TILE = 8
WIDE = 256
BOTH = ("sec", "dom")


def face_rows(face):
    rows = np.arange(NV * 54).reshape(NV * 2, 3, 3, 3)
    return np.take(rows, 0 if face % 2 == 0 else 2, axis=1 + face // 2).reshape(-1)


def picker(faces, unknowns):
    picks = np.zeros((len(faces) * SLOT, unknowns), np.float32)
    for slot, face in enumerate(faces):
        rows = face_rows(face)
        picks[slot * SLOT + np.arange(rows.size), rows] = 1
    return jnp.asarray(picks, jnp.bfloat16)


def kron_parts(sides):
    row = np.arange(SLOT)
    valid = row < NV * NODES
    variable, node = row // NODES, row % NODES
    left = np.zeros((SLOT, NV), np.float32)
    left[row[valid], variable[valid]] = 1
    right = np.zeros((sides * NV, sides * SLOT), np.float32)
    for side in range(sides):
        right[side * NV + variable[valid], side * SLOT + row[valid]] = 1
    same = (node[:, None] == node[None, :]) & valid[:, None] & valid[None, :]
    return (
        jnp.asarray(left, jnp.bfloat16),
        jnp.asarray(right, jnp.bfloat16),
        jnp.asarray(np.concatenate([same, same], axis=1), jnp.float32),
    )


def dot(a, b):
    return jnp.dot(a, b, preferred_element_type=jnp.float32)


VMEM = pl.BlockSpec(memory_space=pltpu.VMEM)


def odd(axis):
    return lax.rem(lax.axis_index(axis), 2) == 1


def trace_kernel(state_ref, picks_ref, late_ref, trace_ref, *head_refs):
    unknowns, count = state_ref.shape
    width = head_refs[0].shape[1]
    early = min(unknowns, WIDE)
    tail = SLOT - late_ref.shape[0] // 6
    for chunk in range(count // WIDE):
        cols = slice(chunk * WIDE, (chunk + 1) * WIDE)
        picked = dot(picks_ref[...], state_ref[:early, cols])
        late = dot(late_ref[...], state_ref[early:, cols])
        rest = SLOT - tail
        for face in range(6):
            first = face * SLOT
            low = picked[first : first + tail].astype(jnp.bfloat16)
            high = (picked[first + tail : first + SLOT] + late[face * rest : (face + 1) * rest]).astype(jnp.bfloat16)
            trace_ref[face, chunk, :tail, :] = low
            trace_ref[face, chunk, tail:, :] = high
    for axis, which in enumerate(BOTH[::-1]):
        flip = odd(which)
        low, high = (trace_ref[2 * axis + side, 0, :, :width] for side in range(2))
        head_refs[2 * axis][...] = jnp.where(flip, low, high)
        head_refs[2 * axis + 1][...] = jnp.where(flip, high, low)


def all_traces(flow_state, head_count):
    unknowns, count = flow_state.shape
    picks = picker(range(6), unknowns)
    early = min(unknowns, WIDE)
    rows = np.concatenate([face_rows(face) for face in range(6)]).reshape(6, -1)
    tail = int(np.nonzero((rows >= early).any(axis=0))[0][0]) // 16 * 16
    late = picks.reshape(6, SLOT, unknowns)[:, tail:, early:].reshape(-1, unknowns - early)
    return pl.pallas_call(
        trace_kernel,
        in_specs=[VMEM] * 3,
        out_specs=[VMEM] * 5,
        out_shape=[jax.ShapeDtypeStruct((6, count // WIDE, SLOT, WIDE), jnp.bfloat16)]
        + [jax.ShapeDtypeStruct((SLOT, head_count), jnp.bfloat16)] * 4,
        compiler_params=pltpu.CompilerParams(vmem_limit_bytes=24 << 20),
        cost_estimate=pl.CostEstimate(flops=1 << 30, bytes_accessed=4 << 20, transcendentals=0),
        name="all_traces",
    )(flow_state, picks[:, :early], late)


def chosen(index, rows):
    row = lax.broadcasted_iota(jnp.int32, (rows, index.shape[1]), 0)
    return jnp.where(row == index, 1.0, 0.0).astype(jnp.bfloat16)


def local_kernel(trace_ref, nbr_ref, volume_ref, lift_ref, jac_ref, left_ref, right_ref, same_ref, out_ref, weights_ref, flux_mat_ref):
    chunks = trace_ref.shape[1]
    spread = dot(left_ref[...], jac_ref[...]).astype(jnp.bfloat16)
    spread = dot(spread, right_ref[...])
    for face in range(6):
        both = spread[:, face * 2 * SLOT : (face + 1) * 2 * SLOT]
        flux_mat_ref[face] = (both * same_ref[...]).astype(jnp.bfloat16)
    unknowns = volume_ref.shape[1]
    values = lift_ref.shape[2]
    first, second, total_width = operand_places(unknowns)
    for direction in range(4):
        weights_ref[direction, :, :unknowns] = volume_ref[direction]
        weights_ref[direction, :, unknowns:] = jnp.zeros((unknowns, total_width - unknowns), jnp.bfloat16)
        if direction < 3:
            weights_ref[direction, :, first : first + values] = lift_ref[2 * direction]
            weights_ref[direction, :, second : second + values] = lift_ref[2 * direction + 1]
    for step in range(chunks):
        here = slice(step * WIDE, (step + 1) * WIDE)
        for face in range(6):
            index = nbr_ref[face : face + 1, here]
            part = lax.shift_right_logical(index, WIDE.bit_length() - 1)
            source = trace_ref[face ^ 1].reshape(chunks * SLOT, WIDE)
            each = dot(source, chosen(jnp.bitwise_and(index, WIDE - 1), WIDE))
            found = jnp.where(part == 0, each[:SLOT], 0.0)
            for chunk in range(1, chunks):
                found = jnp.where(part == chunk, each[chunk * SLOT : (chunk + 1) * SLOT], found)
            out_ref[face, :, here] = found.astype(jnp.bfloat16)


def operand_places(unknowns):
    first = -(-unknowns // 16) * 16
    second = -(-(first + SLOT) // 128) * 128
    return first, second, second + SLOT


def local_traces(traces, face_nbr, volume_ops, lift_ops, jac):
    faces, chunks, slot, wide = traces.shape
    unknowns = volume_ops.shape[1]
    args = (traces, face_nbr, volume_ops, lift_ops, jac, *kron_parts(12))
    return pl.pallas_call(
        local_kernel,
        in_specs=[VMEM] * len(args),
        out_specs=[VMEM] * 3,
        out_shape=[
            jax.ShapeDtypeStruct((faces, slot, chunks * wide), jnp.bfloat16),
            jax.ShapeDtypeStruct((4, unknowns, operand_places(unknowns)[2]), jnp.bfloat16),
            jax.ShapeDtypeStruct((6, SLOT, 2 * SLOT), jnp.bfloat16),
        ],
        compiler_params=pltpu.CompilerParams(vmem_limit_bytes=24 << 20),
        cost_estimate=pl.CostEstimate(flops=2 << 30, bytes_accessed=4 << 20, transcendentals=0),
        name="local_traces",
    )(*args)


def flow_kernel(
    state_ref, nbr_ref, trace_ref, local_ref, partner0, other0, partner1, other1, weights_ref, flux_mat_ref,
    out_ref, remote_ref,
):
    unknowns, count = state_ref.shape
    first, second, height = operand_places(unknowns)
    for axis, (partner, other, which) in enumerate(((partner0, other0, "dom"), (partner1, other1, "sec"))):
        flip = odd(which)
        remote_ref[2 * axis] = jnp.where(flip, partner[...], other[...])
        remote_ref[2 * axis + 1] = jnp.where(flip, other[...], partner[...])

    def some(step, carry):
        here = pl.ds(pl.multiple_of(step * WIDE, WIDE), WIDE)
        fluxes = []
        for face in range(6):
            found = local_ref[face, :, here]
            if face < 4:
                index = nbr_ref[face : face + 1, here] - count
                found += dot(remote_ref[face], chosen(index, remote_ref.shape[2])).astype(jnp.bfloat16)
            sides = jnp.concatenate([trace_ref[face, step], found], axis=0)
            fluxes.append(dot(flux_mat_ref[face], sides).astype(jnp.bfloat16))
        own = state_ref[:, here]
        own_padded = jnp.concatenate([own, jnp.zeros((first - unknowns, WIDE), jnp.bfloat16)], axis=0)
        gap = jnp.zeros((second - first - SLOT, WIDE), jnp.bfloat16)
        for direction in range(4):
            if direction < 3:
                operand = jnp.concatenate([own_padded, fluxes[2 * direction], gap, fluxes[2 * direction + 1]], axis=0)
                out_ref[direction, :, here] = dot(weights_ref[direction], operand)
            else:
                out_ref[direction, :, here] = dot(weights_ref[direction, :, :unknowns], own)
        return carry

    lax.fori_loop(0, count // WIDE, some, 0)


def flow_parts(flow_state, face_nbr, traces, local, remotes, weights, flux_mat):
    unknowns, count = flow_state.shape
    args = (flow_state, face_nbr, traces, local, *remotes, weights, flux_mat)
    return pl.pallas_call(
        flow_kernel,
        in_specs=[VMEM] * len(args),
        out_specs=VMEM,
        out_shape=jax.ShapeDtypeStruct((4, unknowns, count), jnp.float32),
        scratch_shapes=[pltpu.VMEM((4, *remotes[0].shape), jnp.bfloat16)],
        compiler_params=pltpu.CompilerParams(vmem_limit_bytes=32 << 20),
        cost_estimate=pl.CostEstimate(flops=3 << 30, bytes_accessed=4 << 20, transcendentals=0),
        name="flow_parts",
    )(*args)


def total(tiles):
    tile = functools.reduce(jnp.add, tiles)
    tile = jnp.sum(jnp.sum(tile, axis=0, keepdims=True), axis=1, keepdims=True)
    return jnp.broadcast_to(tile, (TILE, 128))


def wall_kernel(
    masks, rows, own_rows,
    near_ref, far_ref, base_ref, follow_ref, anchor_ref, parts_ref, residual_ref, disp_ref,
    disp, resid, applied, search, image, diag,
):
    comps = 3
    tiles = rows // TILE
    me = lax.axis_index(BOTH)

    def strided(block):
        first = block * TILE
        return pl.ds((first % tiles) * TILE + first // tiles, TILE, stride=TILE)

    each = 3 * comps * own_rows
    half = near_ref.shape[0] // each
    for pair in range(half):
        ref, at = (near_ref, pair) if pair < half // 2 else (far_ref, pair - half // 2)
        both = ref[2 * at * each : 2 * (at + 1) * each, :].astype(jnp.float32)
        for slot in range(2):
            device = jnp.bitwise_xor(me, masks[2 * pair + slot])
            upper, lower, stiff = (both[slot * each + k * comps * own_rows :][: comps * own_rows] for k in range(3))
            load = upper + lower
            for block in range(own_rows // TILE):
                to = strided(device * (own_rows // TILE) + block)
                for c in range(comps):
                    first = c * own_rows + block * TILE
                    resid[c, to, :] = load[first : first + TILE]
                    diag[c, to, :] = 4.0 + stiff[first : first + TILE]

    lane = lax.broadcasted_iota(jnp.int32, (TILE, 128), 1)
    sub = lax.broadcasted_iota(jnp.int32, (TILE, 128), 0)
    group = 32 if tiles % 32 == 0 else 8
    zero = jnp.zeros((TILE, 128), jnp.float32)

    def at(tile):
        return pl.ds(tile * TILE if isinstance(tile, int) else pl.multiple_of(tile * TILE, TILE), TILE)

    def sweep(renew):
        norms, energies = [], []
        for c in range(comps):
            above = jnp.where(sub == 0, 0.0, pltpu.roll(renew(c, tiles - 1, False), 1, 0))

            def operate(tile, above, value, below, c=c):
                beside = above + below
                beside += jnp.where(lane == 0, 0.0, pltpu.roll(value, 1, 1))
                beside += jnp.where(lane == 127, 0.0, pltpu.roll(value, 127, 1))
                result = diag[c, at(tile), :] * value - beside
                applied[c, at(tile), :] = result
                return value * value, value * result

            def some(chunk, carry, c=c):
                above, value, norm, energy = carry
                norm, energy = [norm, zero], [energy, zero]
                for k in range(group):
                    tile = chunk * group + k + 1
                    below = renew(c, tile, True)
                    terms = operate(tile - 1, above, value, below)
                    norm[k % 2] += terms[0]
                    energy[k % 2] += terms[1]
                    above, value = value, below
                return above, value, norm[0] + norm[1], energy[0] + energy[1]

            first = value = renew(c, 0, True)
            norm = energy = zero
            if tiles > group:
                above, value, norm, energy = lax.fori_loop(0, tiles // group - 1, some, (above, value, norm, energy))
            norm, energy = [norm, zero], [energy, zero]
            for tile in range(tiles - group + 1, tiles + 1):
                if tile < tiles:
                    below = renew(c, tile, True)
                else:
                    below = jnp.where(sub == TILE - 1, 0.0, pltpu.roll(first, TILE - 1, 0))
                terms = operate(tile - 1, above, value, below)
                norm[tile % 2] += terms[0]
                energy[tile % 2] += terms[1]
                above, value = value, below
            norms += norm
            energies += energy
        return total(norms), total(energies)

    def begin(c, tile, keep):
        return resid[c, at(tile), :]

    def advance(step_size, ratio, last_step=None, first=False):
        def renew(c, tile, keep):
            value = resid[c, at(tile), :]
            toward, moved = value, applied[c, at(tile), :]
            if not first:
                before = search[c, at(tile), :]
                toward += ratio * before
                moved += ratio * image[c, at(tile), :]
            value -= step_size * moved
            if keep:
                search[c, at(tile), :] = toward
                image[c, at(tile), :] = moved
                resid[c, at(tile), :] = value
                if last_step is not None:
                    disp[c, at(tile), :] += last_step * before + step_size * toward
            return value

        return renew

    def sizes(norm, energy, last_norm, last_curve):
        ratio = norm / last_norm
        curve = energy - ratio * ratio * last_curve
        return norm / curve, ratio, curve

    norm, curve = sweep(begin)
    step_size = norm / curve
    last_norm, last_curve, last_step = norm, curve, step_size
    norm, energy = sweep(advance(step_size, None, first=True))

    def clear(tile, carry):
        for c in range(comps):
            disp[c, at(tile), :] = zero
        return carry

    lax.fori_loop(0, tiles, clear, 0, unroll=8)

    def two(position, carry):
        norm, energy, last_norm, last_curve, last_step = carry
        step_size, ratio, curve = sizes(norm, energy, last_norm, last_curve)
        last_norm = norm
        norm, energy = sweep(advance(step_size, ratio, last_step))
        step_size, ratio, curve = sizes(norm, energy, last_norm, curve)
        last_norm = norm
        norm, energy = sweep(advance(step_size, ratio))
        return norm, energy, last_norm, curve, step_size

    assert ITERS % 2 == 0
    carry = lax.fori_loop(0, ITERS // 2 - 1, two, (norm, energy, last_norm, last_curve, last_step))
    norm, energy, last_norm, last_curve, last_step = carry
    step_size, ratio, curve = sizes(norm, energy, last_norm, last_curve)

    def finish(tile, carry):
        for c in range(comps):
            before = search[c, at(tile), :]
            toward = resid[c, at(tile), :] + ratio * before
            disp[c, at(tile), :] += last_step * before + step_size * toward
        return carry

    lax.fori_loop(0, tiles, finish, 0, unroll=8)

    for block in range(own_rows // TILE):
        for c in range(comps):
            disp_ref[c, block * TILE : (block + 1) * TILE, :] = disp[c, strided(me * (own_rows // TILE) + block), :]

    anchor = anchor_ref[...]
    count = anchor.shape[1]
    row = anchor // 128
    column = anchor - row * 128
    upper = row // tiles
    place = (row - upper * tiles) * TILE + upper
    pick = jnp.where(lax.broadcasted_iota(jnp.int32, (128, count), 0) == column, 1.0, 0.0).astype(jnp.bfloat16)
    pick = jnp.concatenate([pick, pick], axis=0)
    some_rows = 128
    row_of = lax.broadcasted_iota(jnp.int32, (some_rows, count), 0)

    def look(chunk, sums):
        first = pl.multiple_of(chunk * some_rows, some_rows)
        hit = row_of == place - first
        out = []
        for c in range(comps):
            value = disp[c, pl.ds(first, some_rows), :]
            coarse = value.astype(jnp.bfloat16)
            fine = (value - coarse.astype(jnp.float32)).astype(jnp.bfloat16)
            found = dot(jnp.concatenate([coarse, fine], axis=1), pick)
            found = jnp.where(hit, found, 0.0).reshape(some_rows // TILE, TILE, count)
            out.append(sums[c] + jnp.sum(found, axis=0))
        return tuple(out)

    sums = lax.fori_loop(0, rows // some_rows, look, (jnp.zeros((TILE, count), jnp.float32),) * comps)
    follow = follow_ref[...]
    geometry = [
        base_ref[c : c + 1, :] * jnp.exp(follow * jnp.sum(sums[c], axis=0, keepdims=True)) for c in range(comps)
    ]
    geometry.append(base_ref[comps : comps + 1, :])
    unknowns = residual_ref.shape[0]
    for first in range(0, unknowns, 16):
        some = slice(first, min(first + 16, unknowns))
        value = geometry[0] * parts_ref[0, some, :]
        for direction in range(1, 4):
            value += geometry[direction] * parts_ref[direction, some, :]
        residual_ref[some, :] = value.astype(jnp.bfloat16)


def wall_and_residual(near, far, masks, base_geometry, anchor_weight, wall_anchor, parts, own_rows):
    rows = own_rows * len(masks)
    _, unknowns, count = parts.shape
    field = pltpu.VMEM((3, rows, 128), jnp.float32)
    return pl.pallas_call(
        functools.partial(wall_kernel, masks, rows, own_rows),
        in_specs=[VMEM] * 6,
        out_specs=[VMEM] * 2,
        out_shape=[
            jax.ShapeDtypeStruct((unknowns, count), jnp.bfloat16),
            jax.ShapeDtypeStruct((3, own_rows, 128), jnp.float32),
        ],
        scratch_shapes=[
            field,
            field,
            field,
            field,
            field,
            field,
        ],
        compiler_params=pltpu.CompilerParams(vmem_limit_bytes=(16 << 20) + 16 * rows * 3 * 128 * 4),
        cost_estimate=pl.CostEstimate(flops=4 << 30, bytes_accessed=8 << 20, transcendentals=0),
        name="wall_and_residual",
    )(near, far, base_geometry, anchor_weight[None, :], wall_anchor[None, :], parts)


def paired(x, axis, offset):
    peers = lax.axis_size(axis)
    pairs = [((i + offset) % peers, (i + offset + 1) % peers) for i in range(0, peers, 2)]
    return lax.ppermute(x, axis, pairs + [pair[::-1] for pair in pairs])


def gather_stages(mesh):
    def bits(axis):
        assert mesh.shape[axis] & (mesh.shape[axis] - 1) == 0
        return [(axis, 1 << b) for b in reversed(range(mesh.shape[axis].bit_length() - 1))]

    return bits("dom") + bits("sec")


def on_device(
    stages, n_dom,
    flow_state, base_geometry, anchor_weight, wall_anchor, face_nbr, volume_ops, lift_ops, face_jac, wall_load, wall_stiff,
):
    own_rows, width = wall_load.shape[1:]
    upper = lax.reduce_precision(wall_load, 8, 7)
    wall = jnp.concatenate([upper, wall_load - upper, wall_stiff], axis=0).astype(jnp.bfloat16)
    wall = wall.reshape(9 * own_rows, width)
    masks = [0]
    for axis, bit in stages:
        masks += [m ^ (bit * n_dom if axis == "sec" else bit) for m in masks]

    def sent(wall, position):
        axis, bit = stages[position]
        return lax.ppermute(wall, axis, [(i, i ^ bit) for i in range(lax.axis_size(axis))])

    barrier = lax.optimization_barrier
    far = sent(wall, 0)
    head_count = flow_state.shape[1] // 8
    traces, *heads = all_traces(flow_state, head_count)
    far, traces, heads = barrier((far, traces, heads))
    wall = jnp.concatenate([wall, far], axis=0)
    far = sent(wall, 1)
    remotes = [None] * 4
    remotes[2] = paired(heads[2], "sec", 0)
    remotes[1] = paired(heads[1], "dom", 1)
    far, heads, remotes[2], volume_ops, lift_ops, face_jac = barrier((far, heads, remotes[2], volume_ops, lift_ops, face_jac))
    wall = jnp.concatenate([wall, far], axis=0)
    far = sent(wall, 2)
    remotes[0] = paired(heads[0], "dom", 0)
    remotes[3] = paired(heads[3], "sec", 1)
    jac = face_jac.transpose(2, 0, 1, 3).reshape(NV, 12 * NV)
    local, weights, flux_mat = local_traces(traces, face_nbr, volume_ops, lift_ops, jac)
    far, remotes, local = barrier((far, remotes, local))
    wall = jnp.concatenate([wall, far], axis=0)
    far = sent(wall, 3)
    parts = flow_parts(flow_state, face_nbr, traces, local, remotes, weights, flux_mat)
    far, parts = barrier((far, parts))
    for position in range(4, len(stages)):
        wall = jnp.concatenate([wall, far], axis=0)
        far = sent(wall, position)
    return wall_and_residual(wall, far, masks, base_geometry, anchor_weight, wall_anchor, parts, own_rows)


def solution(mesh):
    return jax.shard_map(
        functools.partial(on_device, gather_stages(mesh), mesh.shape["dom"]),
        mesh=mesh,
        in_specs=(
            P(None, BOTH),
            P(None, BOTH),
            P(BOTH),
            P(BOTH),
            P(None, BOTH),
            P(),
            P(),
            P(),
            P(None, BOTH, None),
            P(None, BOTH, None),
        ),
        out_specs=(P(None, BOTH), P(None, BOTH, None)),
        check_vma=False,
    )
```

```python
import functools

import jax
import jax.numpy as jnp
import numpy as np
from jax import lax
from jax.experimental import pallas as pl
from jax.experimental.pallas import tpu as pltpu
from jax.sharding import PartitionSpec as P

NV = 5
ITERS = 8
NODES = 18
SLOT = 96
TILE = 8
WIDE = 256
BOTH = ("sec", "dom")


def face_rows(face):
    rows = np.arange(NV * 54).reshape(NV * 2, 3, 3, 3)
    return np.take(rows, 0 if face % 2 == 0 else 2, axis=1 + face // 2).reshape(-1)


def kron_parts(sides):
    row = np.arange(SLOT)
    valid = row < NV * NODES
    variable, node = row // NODES, row % NODES
    left = np.zeros((SLOT, NV), np.float32)
    left[row[valid], variable[valid]] = 1
    right = np.zeros((sides * NV, sides * SLOT), np.float32)
    for side in range(sides):
        right[side * NV + variable[valid], side * SLOT + row[valid]] = 1
    same = (node[:, None] == node[None, :]) & valid[:, None] & valid[None, :]
    return (
        jnp.asarray(left, jnp.bfloat16),
        jnp.asarray(right, jnp.bfloat16),
        jnp.asarray(np.concatenate([same, same], axis=1), jnp.float32),
    )


def dot(a, b):
    return jnp.dot(a, b, preferred_element_type=jnp.float32)


VMEM = pl.BlockSpec(memory_space=pltpu.VMEM)

HBM = pl.BlockSpec(memory_space=pltpu.HBM)


def odd(axis):
    return lax.rem(lax.axis_index(axis), 2) == 1


def picks(face, rows, columns):
    shape = (rows.stop - rows.start, columns.stop - columns.start)
    row = lax.broadcasted_iota(jnp.int32, shape, 0) + rows.start
    column = lax.broadcasted_iota(jnp.int32, shape, 1) + columns.start
    group = lax.shift_right_logical(row * 57, 9)
    inner = row - 9 * group
    upper = lax.shift_right_logical(inner * 11, 5)
    side = 2 * (face % 2)
    if face // 2 == 0:
        within = 9 * side + inner
    elif face // 2 == 1:
        within = 9 * upper + 3 * side + inner - 3 * upper
    else:
        within = 3 * inner + side
    hit = (column == 27 * group + within) & (row < NV * NODES)
    return jnp.where(hit, 1.0, 0.0).astype(jnp.bfloat16)


def trace_kernel(state_ref, trace_ref, *refs):
    head_refs = refs[:4]
    main_ref, late_ref = refs[4:]
    unknowns, count = state_ref.shape
    width = head_refs[0].shape[1]
    early = min(unknowns, WIDE)
    tail = late_rows(unknowns)
    rest = SLOT - tail
    for face in range(6):
        main_ref[face * SLOT : (face + 1) * SLOT, :] = picks(face, range(SLOT), range(early))
        late_ref[face * rest : (face + 1) * rest, :] = picks(face, range(tail, SLOT), range(early, unknowns))
    for chunk in range(count // WIDE):
        cols = slice(chunk * WIDE, (chunk + 1) * WIDE)
        main = dot(main_ref[...], state_ref[:early, cols])
        late = dot(late_ref[...], state_ref[early:, cols])
        for face in range(6):
            first = face * SLOT
            trace_ref[face, chunk, :tail, :] = main[first : first + tail].astype(jnp.bfloat16)
            both = main[first + tail : first + SLOT] + late[face * rest : (face + 1) * rest]
            trace_ref[face, chunk, tail:, :] = both.astype(jnp.bfloat16)
    for axis, which in enumerate(BOTH[::-1]):
        flip = odd(which)
        low, high = (trace_ref[2 * axis + side, 0, :, :width] for side in range(2))
        head_refs[2 * axis][...] = jnp.where(flip, low, high)
        head_refs[2 * axis + 1][...] = jnp.where(flip, high, low)


def late_rows(unknowns):
    rows = np.stack([face_rows(face) for face in range(6)])
    return int(np.nonzero((rows >= min(unknowns, WIDE)).any(axis=0))[0][0]) // 16 * 16


def all_traces(flow_state, head_count):
    unknowns, count = flow_state.shape
    early = min(unknowns, WIDE)
    shapes = [(6, count // WIDE, SLOT, WIDE)] + [(SLOT, head_count)] * 4
    return pl.pallas_call(
        trace_kernel,
        in_specs=[VMEM],
        out_specs=[VMEM] * 5,
        out_shape=[jax.ShapeDtypeStruct(shape, jnp.bfloat16) for shape in shapes],
        scratch_shapes=[
            pltpu.VMEM((6 * SLOT, early), jnp.bfloat16),
            pltpu.VMEM((6 * (SLOT - late_rows(unknowns)), unknowns - early), jnp.bfloat16),
        ],
        compiler_params=pltpu.CompilerParams(vmem_limit_bytes=24 << 20),
        cost_estimate=pl.CostEstimate(flops=1 << 30, bytes_accessed=4 << 20, transcendentals=0),
        name="all_traces",
    )(flow_state)


def chosen(index, rows):
    row = lax.broadcasted_iota(jnp.int32, (rows, index.shape[1]), 0)
    return jnp.where(row == index, 1.0, 0.0).astype(jnp.bfloat16)


def local_kernel(trace_ref, nbr_ref, volume_ref, lift_ref, jac_ref, left_ref, right_ref, same_ref, out_ref, weights_ref, flux_mat_ref):
    chunks = trace_ref.shape[1]
    spread = dot(left_ref[...], jac_ref[...]).astype(jnp.bfloat16)
    spread = dot(spread, right_ref[...])
    for face in range(6):
        both = spread[:, face * 2 * SLOT : (face + 1) * 2 * SLOT]
        flux_mat_ref[face] = (both * same_ref[...]).astype(jnp.bfloat16)
    unknowns = volume_ref.shape[1]
    values = lift_ref.shape[2]
    first, second, total_width = operand_places(unknowns)
    for direction in range(4):
        weights_ref[direction, :, :unknowns] = volume_ref[direction]
        weights_ref[direction, :, unknowns:] = jnp.zeros((unknowns, total_width - unknowns), jnp.bfloat16)
        if direction < 3:
            weights_ref[direction, :, first : first + values] = lift_ref[2 * direction]
            weights_ref[direction, :, second : second + values] = lift_ref[2 * direction + 1]
    for step in range(chunks):
        here = slice(step * WIDE, (step + 1) * WIDE)
        for face in range(6):
            index = nbr_ref[face : face + 1, here]
            part = lax.shift_right_logical(index, WIDE.bit_length() - 1)
            source = trace_ref[face ^ 1].reshape(chunks * SLOT, WIDE)
            each = dot(source, chosen(jnp.bitwise_and(index, WIDE - 1), WIDE))
            found = jnp.where(part == 0, each[:SLOT], 0.0)
            for chunk in range(1, chunks):
                found = jnp.where(part == chunk, each[chunk * SLOT : (chunk + 1) * SLOT], found)
            out_ref[face, :, here] = found.astype(jnp.bfloat16)


def operand_places(unknowns):
    first = -(-unknowns // 16) * 16
    second = -(-(first + SLOT) // 128) * 128
    return first, second, second + SLOT


def local_traces(traces, face_nbr, volume_ops, lift_ops, jac):
    faces, chunks, slot, wide = traces.shape
    unknowns = volume_ops.shape[1]
    args = (traces, face_nbr, volume_ops, lift_ops, jac, *kron_parts(12))
    return pl.pallas_call(
        local_kernel,
        in_specs=[VMEM] * len(args),
        out_specs=[VMEM] * 3,
        out_shape=[
            jax.ShapeDtypeStruct((faces, slot, chunks * wide), jnp.bfloat16),
            jax.ShapeDtypeStruct((4, unknowns, operand_places(unknowns)[2]), jnp.bfloat16),
            jax.ShapeDtypeStruct((6, SLOT, 2 * SLOT), jnp.bfloat16),
        ],
        compiler_params=pltpu.CompilerParams(vmem_limit_bytes=24 << 20),
        cost_estimate=pl.CostEstimate(flops=2 << 30, bytes_accessed=4 << 20, transcendentals=0),
        name="local_traces",
    )(*args)


def flow_kernel(
    start, state_ref, nbr_ref, trace_ref, local_ref, partner0, other0, partner1, other1, weights_ref, flux_mat_ref,
    out_ref, remote_ref,
):
    unknowns, count = state_ref.shape
    first, second, height = operand_places(unknowns)
    for axis, (partner, other, which) in enumerate(((partner0, other0, "dom"), (partner1, other1, "sec"))):
        flip = odd(which)
        remote_ref[2 * axis] = jnp.where(flip, partner[...], other[...])
        remote_ref[2 * axis + 1] = jnp.where(flip, other[...], partner[...])

    def some(pair, carry):
        places = [pair * 2 + k for k in range(2)]
        wheres = [pl.ds(pl.multiple_of((start + p) * WIDE, WIDE), WIDE) for p in places]
        found = {}
        for k, here in enumerate(wheres):
            for face in range(6):
                found[k, face] = local_ref[face, :, here]
                if face < 4:
                    index = nbr_ref[face : face + 1, here] - count
                    found[k, face] += dot(remote_ref[face], chosen(index, remote_ref.shape[2])).astype(jnp.bfloat16)
        fluxes = {}
        for k, p in enumerate(places):
            for face in range(6):
                sides = jnp.concatenate([trace_ref[face, start + p], found[k, face]], axis=0)
                fluxes[k, face] = dot(flux_mat_ref[face], sides).astype(jnp.bfloat16)
        gap = jnp.zeros((second - first - SLOT, WIDE), jnp.bfloat16)
        for k, p in enumerate(places):
            there = pl.ds(pl.multiple_of(p * WIDE, WIDE), WIDE)
            own = state_ref[:, wheres[k]]
            own_padded = jnp.concatenate([own, jnp.zeros((first - unknowns, WIDE), jnp.bfloat16)], axis=0)
            for direction in range(4):
                if direction < 3:
                    operand = [own_padded, fluxes[k, 2 * direction], gap, fluxes[k, 2 * direction + 1]]
                    out_ref[direction, :, there] = dot(weights_ref[direction], jnp.concatenate(operand, axis=0))
                else:
                    out_ref[direction, :, there] = dot(weights_ref[direction, :, :unknowns], own)
        return carry

    for pair in range(out_ref.shape[2] // WIDE // 2):
        some(pair, 0)


def flow_parts(start, steps, flow_state, face_nbr, traces, local, remotes, weights, flux_mat):
    unknowns = flow_state.shape[0]
    args = (flow_state, face_nbr, traces, local, *remotes, weights, flux_mat)
    return pl.pallas_call(
        functools.partial(flow_kernel, start),
        in_specs=[VMEM] * len(args),
        out_specs=VMEM,
        out_shape=jax.ShapeDtypeStruct((4, unknowns, steps * WIDE), jnp.float32),
        scratch_shapes=[pltpu.VMEM((4, *remotes[0].shape), jnp.bfloat16)],
        compiler_params=pltpu.CompilerParams(vmem_limit_bytes=32 << 20),
        cost_estimate=pl.CostEstimate(flops=3 << 30, bytes_accessed=4 << 20, transcendentals=0),
        name="flow_parts",
    )(*args)


def total(tiles):
    tile = functools.reduce(jnp.add, tiles)
    tile = jnp.sum(jnp.sum(tile, axis=0, keepdims=True), axis=1, keepdims=True)
    return jnp.broadcast_to(tile, (TILE, 128))


def wall_kernel(
    masks, kind_bits, rows, own_rows,
    near_ref, far_ref, base_ref, follow_ref, anchor_ref, parts0_ref, parts1_ref, residual_ref, disp_ref,
    disp, resid, applied, search, image, diag,
):
    comps = 3
    tiles = rows // TILE
    me = lax.axis_index(BOTH)
    flip = kind(me, kind_bits) == 1

    def strided(block):
        first = block * TILE
        return pl.ds((first % tiles) * TILE + first // tiles, TILE, stride=TILE)

    each = 3 * comps * own_rows
    half = near_ref.shape[0] // each
    for pair in range(half):
        ref, at = (near_ref, pair) if pair < half // 2 else (far_ref, pair - half // 2)
        both = ref[2 * at * each : 2 * (at + 1) * each, :].astype(jnp.float32)
        for slot in range(2):
            device = jnp.bitwise_xor(me, jnp.where(flip, masks[1][2 * pair + slot], masks[0][2 * pair + slot]))
            upper, lower, stiff = (both[slot * each + k * comps * own_rows :][: comps * own_rows] for k in range(3))
            load = upper + lower
            for block in range(own_rows // TILE):
                to = strided(device * (own_rows // TILE) + block)
                for c in range(comps):
                    first = c * own_rows + block * TILE
                    resid[c, to, :] = load[first : first + TILE]
                    diag[c, to, :] = 4.0 + stiff[first : first + TILE]

    lane = lax.broadcasted_iota(jnp.int32, (TILE, 128), 1)
    sub = lax.broadcasted_iota(jnp.int32, (TILE, 128), 0)
    group = 32 if tiles % 32 == 0 else 8
    zero = jnp.zeros((TILE, 128), jnp.float32)

    def at(tile):
        return pl.ds(tile * TILE if isinstance(tile, int) else pl.multiple_of(tile * TILE, TILE), TILE)

    def sweep(renew):
        norms, energies = [], []
        for c in range(comps):
            above = jnp.where(sub == 0, 0.0, pltpu.roll(renew(c, tiles - 1, False), 1, 0))

            def operate(tile, above, value, below, c=c):
                beside = above + below
                beside += jnp.where(lane == 0, 0.0, pltpu.roll(value, 1, 1))
                beside += jnp.where(lane == 127, 0.0, pltpu.roll(value, 127, 1))
                result = diag[c, at(tile), :] * value - beside
                applied[c, at(tile), :] = result
                return value * value, value * result

            def some(chunk, carry, c=c):
                above, value, norm, energy = carry
                norm, energy = [norm, zero], [energy, zero]
                for k in range(group):
                    tile = chunk * group + k + 1
                    below = renew(c, tile, True)
                    terms = operate(tile - 1, above, value, below)
                    norm[k % 2] += terms[0]
                    energy[k % 2] += terms[1]
                    above, value = value, below
                return above, value, norm[0] + norm[1], energy[0] + energy[1]

            first = value = renew(c, 0, True)
            norm = energy = zero
            if tiles > group:
                above, value, norm, energy = lax.fori_loop(0, tiles // group - 1, some, (above, value, norm, energy))
            norm, energy = [norm, zero], [energy, zero]
            for tile in range(tiles - group + 1, tiles + 1):
                if tile < tiles:
                    below = renew(c, tile, True)
                else:
                    below = jnp.where(sub == TILE - 1, 0.0, pltpu.roll(first, TILE - 1, 0))
                terms = operate(tile - 1, above, value, below)
                norm[tile % 2] += terms[0]
                energy[tile % 2] += terms[1]
                above, value = value, below
            norms += norm
            energies += energy
        return total(norms), total(energies)

    def begin(c, tile, keep):
        return resid[c, at(tile), :]

    def advance(step_size, ratio, last_step=None, first=False):
        def renew(c, tile, keep):
            value = resid[c, at(tile), :]
            toward, moved = value, applied[c, at(tile), :]
            if not first:
                before = search[c, at(tile), :]
                toward += ratio * before
                moved += ratio * image[c, at(tile), :]
            value -= step_size * moved
            if keep:
                search[c, at(tile), :] = toward
                image[c, at(tile), :] = moved
                resid[c, at(tile), :] = value
                if last_step is not None:
                    disp[c, at(tile), :] += last_step * before + step_size * toward
            return value

        return renew

    def sizes(norm, energy, last_norm, last_curve):
        ratio = norm / last_norm
        curve = energy - ratio * ratio * last_curve
        return norm / curve, ratio, curve

    norm, curve = sweep(begin)
    step_size = norm / curve
    last_norm, last_curve, last_step = norm, curve, step_size
    norm, energy = sweep(advance(step_size, None, first=True))

    def clear(tile, carry):
        for c in range(comps):
            disp[c, at(tile), :] = zero
        return carry

    lax.fori_loop(0, tiles, clear, 0, unroll=8)

    def two(position, carry):
        norm, energy, last_norm, last_curve, last_step = carry
        step_size, ratio, curve = sizes(norm, energy, last_norm, last_curve)
        last_norm = norm
        norm, energy = sweep(advance(step_size, ratio, last_step))
        step_size, ratio, curve = sizes(norm, energy, last_norm, curve)
        last_norm = norm
        norm, energy = sweep(advance(step_size, ratio))
        return norm, energy, last_norm, curve, step_size

    assert ITERS % 2 == 0
    carry = lax.fori_loop(0, ITERS // 2 - 1, two, (norm, energy, last_norm, last_curve, last_step))
    norm, energy, last_norm, last_curve, last_step = carry
    step_size, ratio, curve = sizes(norm, energy, last_norm, last_curve)

    def finish(tile, carry):
        for c in range(comps):
            before = search[c, at(tile), :]
            toward = resid[c, at(tile), :] + ratio * before
            disp[c, at(tile), :] += last_step * before + step_size * toward
        return carry

    lax.fori_loop(0, tiles, finish, 0, unroll=8)

    for block in range(own_rows // TILE):
        for c in range(comps):
            disp_ref[c, block * TILE : (block + 1) * TILE, :] = disp[c, strided(me * (own_rows // TILE) + block), :]

    anchor = anchor_ref[...]
    count = anchor.shape[1]
    row = anchor // 128
    column = anchor - row * 128
    upper = row // tiles
    place = (row - upper * tiles) * TILE + upper
    pick = jnp.where(lax.broadcasted_iota(jnp.int32, (128, count), 0) == column, 1.0, 0.0).astype(jnp.bfloat16)
    pick = jnp.concatenate([pick, pick], axis=0)
    some_rows = 128
    row_of = lax.broadcasted_iota(jnp.int32, (some_rows, count), 0)

    def look(chunk, sums):
        first = pl.multiple_of(chunk * some_rows, some_rows)
        hit = row_of == place - first
        out = []
        for c in range(comps):
            value = disp[c, pl.ds(first, some_rows), :]
            coarse = value.astype(jnp.bfloat16)
            fine = (value - coarse.astype(jnp.float32)).astype(jnp.bfloat16)
            found = dot(jnp.concatenate([coarse, fine], axis=1), pick)
            found = jnp.where(hit, found, 0.0).reshape(some_rows // TILE, TILE, count)
            out.append(sums[c] + jnp.sum(found, axis=0))
        return tuple(out)

    sums = (jnp.zeros((TILE, count), jnp.float32),) * comps
    sums = lax.fori_loop(0, rows // some_rows, look, sums, unroll=rows // some_rows <= 4)
    follow = follow_ref[...]
    geometry = [
        base_ref[c : c + 1, :] * jnp.exp(follow * jnp.sum(sums[c], axis=0, keepdims=True)) for c in range(comps)
    ]
    geometry.append(base_ref[comps : comps + 1, :])
    unknowns = residual_ref.shape[0]
    begin = 0
    for parts_ref in (parts0_ref, parts1_ref):
        cols = slice(begin, begin + parts_ref.shape[2])
        begin = cols.stop
        for first in range(0, unknowns, 16):
            some = slice(first, min(first + 16, unknowns))
            value = geometry[0][:, cols] * parts_ref[0, some, :]
            for direction in range(1, 4):
                value += geometry[direction][:, cols] * parts_ref[direction, some, :]
            residual_ref[some, cols] = value.astype(jnp.bfloat16)


def wall_and_residual(near, far, masks, kind_bits, base_geometry, anchor_weight, wall_anchor, parts, own_rows):
    rows = own_rows * len(masks[0])
    unknowns, count = parts[0].shape[1], anchor_weight.shape[0]
    field = pltpu.VMEM((3, rows, 128), jnp.float32)
    return pl.pallas_call(
        functools.partial(wall_kernel, masks, kind_bits, rows, own_rows),
        in_specs=[VMEM] * 7,
        out_specs=[VMEM] * 2,
        out_shape=[
            jax.ShapeDtypeStruct((unknowns, count), jnp.bfloat16),
            jax.ShapeDtypeStruct((3, own_rows, 128), jnp.float32),
        ],
        scratch_shapes=[
            field,
            field,
            field,
            field,
            field,
            field,
        ],
        compiler_params=pltpu.CompilerParams(vmem_limit_bytes=(16 << 20) + 16 * rows * 3 * 128 * 4),
        cost_estimate=pl.CostEstimate(flops=4 << 30, bytes_accessed=8 << 20, transcendentals=0),
        name="wall_and_residual",
    )(near, far, base_geometry, anchor_weight[None, :], wall_anchor[None, :], *parts)


def paired(x, axis, offset):
    peers = lax.axis_size(axis)
    pairs = [((i + offset) % peers, (i + offset + 1) % peers) for i in range(0, peers, 2)]
    return lax.ppermute(x, axis, pairs + [pair[::-1] for pair in pairs])


def gather_stages(mesh):
    n_sec, n_dom = mesh.shape["sec"], mesh.shape["dom"]
    assert n_sec & (n_sec - 1) == 0 and n_dom & (n_dom - 1) == 0 and n_sec > 1
    bits = [1 << b for b in range((n_sec * n_dom).bit_length() - 1)]
    inner, outer = bits[: n_dom.bit_length() - 1], bits[n_dom.bit_length() :]
    order = inner[::-1] + outer[::-1]
    first = [bit ^ n_dom for bit in order]
    second = first[:-2] + first[-2:][::-1]
    return (first + [n_dom], second + [n_dom]), order[-2:] + [n_dom]


def kind(device, bits):
    return sum(device // bit % 2 for bit in bits) % 2


def on_device(
    stages, kind_bits,
    flow_state, base_geometry, anchor_weight, wall_anchor, face_nbr, volume_ops, lift_ops, face_jac, wall_load, wall_stiff,
):
    own_rows, width = wall_load.shape[1:]
    wall = jnp.concatenate([wall_load, wall_load, wall_stiff], axis=0).reshape(9 * own_rows, width)
    third = lax.broadcasted_iota(jnp.int32, wall.shape, 0) // (3 * own_rows)
    wall = jnp.where(third == 1, wall - lax.reduce_precision(wall, 8, 7), wall).astype(jnp.bfloat16)
    masks = []
    for bits in stages:
        masks.append([0])
        for bit in bits[:-1]:
            masks[-1] += [m ^ bit for m in masks[-1]]
    masks = [ours + [m ^ stages[0][-1] for m in theirs] for ours, theirs in (masks, masks[::-1])]
    devices = lax.axis_size(BOTH)

    def sent(wall, position):
        pairs = [(i, i ^ stages[kind(i, kind_bits)][position]) for i in range(devices)]
        return lax.ppermute(wall, BOTH, pairs)

    barrier = lax.optimization_barrier
    far = sent(wall, 0)
    head_count = flow_state.shape[1] // 8
    traces, *heads = all_traces(flow_state, head_count)
    far, heads = barrier((far, heads))
    wall = jnp.concatenate([wall, far], axis=0)
    far = sent(wall, 1)
    remotes = [None] * 4
    remotes[2] = paired(heads[2], "sec", 0)
    remotes[0] = paired(heads[0], "dom", 0)
    far, heads = barrier((far, heads))
    wall = jnp.concatenate([wall, far], axis=0)
    far = sent(wall, 2)
    remotes[1] = paired(heads[1], "dom", 1)
    remotes[3] = paired(heads[3], "sec", 1)
    far, traces, volume_ops, face_jac, remotes[0], remotes[2] = barrier((far, traces, volume_ops, face_jac, remotes[0], remotes[2]))
    wall = jnp.concatenate([wall, far], axis=0)
    jac = face_jac.transpose(2, 0, 1, 3).reshape(NV, 12 * NV)
    far = sent(wall, 3)
    local, weights, flux_mat = local_traces(traces, face_nbr, volume_ops, lift_ops, jac)
    chunks = traces.shape[1]
    halves = []
    halves.append(flow_parts(0, chunks // 2, flow_state, face_nbr, traces, local, remotes, weights, flux_mat))
    far, local, halves = barrier((far, local, halves))
    for position in range(4, len(stages[0])):
        wall = jnp.concatenate([wall, far], axis=0)
        far = sent(wall, position)
    halves.append(flow_parts(chunks // 2, chunks // 2, flow_state, face_nbr, traces, local, remotes, weights, flux_mat))
    return wall_and_residual(wall, far, masks, kind_bits, base_geometry, anchor_weight, wall_anchor, halves, own_rows)


def solution(mesh):
    return jax.shard_map(
        functools.partial(on_device, *gather_stages(mesh)),
        mesh=mesh,
        in_specs=(
            P(None, BOTH),
            P(None, BOTH),
            P(BOTH),
            P(BOTH),
            P(None, BOTH),
            P(),
            P(),
            P(),
            P(None, BOTH, None),
            P(None, BOTH, None),
        ),
        out_specs=(P(None, BOTH), P(None, BOTH, None)),
        check_vma=False,
    )
```

```python
import functools

import jax
import jax.numpy as jnp
import numpy as np
from jax import lax
from jax.experimental import pallas as pl
from jax.experimental.pallas import tpu as pltpu
from jax.sharding import PartitionSpec as P

NV = 5
ITERS = 8
NODES = 18
SLOT = 96
TILE = 8
WIDE = 256
BOTH = ("sec", "dom")


def face_rows(face):
    rows = np.arange(NV * 54).reshape(NV * 2, 3, 3, 3)
    return np.take(rows, 0 if face % 2 == 0 else 2, axis=1 + face // 2).reshape(-1)


def kron_parts(sides):
    row = np.arange(SLOT)
    valid = row < NV * NODES
    variable, node = row // NODES, row % NODES
    left = np.zeros((SLOT, NV), np.float32)
    left[row[valid], variable[valid]] = 1
    right = np.zeros((sides * NV, sides * SLOT), np.float32)
    for side in range(sides):
        right[side * NV + variable[valid], side * SLOT + row[valid]] = 1
    same = (node[:, None] == node[None, :]) & valid[:, None] & valid[None, :]
    return (
        jnp.asarray(left, jnp.bfloat16),
        jnp.asarray(right, jnp.bfloat16),
        jnp.asarray(np.concatenate([same, same], axis=1), jnp.float32),
    )


def dot(a, b):
    return jnp.dot(a, b, preferred_element_type=jnp.float32)


VMEM = pl.BlockSpec(memory_space=pltpu.VMEM)

HBM = pl.BlockSpec(memory_space=pltpu.HBM)


def odd(axis):
    return lax.rem(lax.axis_index(axis), 2) == 1


def picks(face, rows, columns):
    shape = (rows.stop - rows.start, columns.stop - columns.start)
    row = lax.broadcasted_iota(jnp.int32, shape, 0) + rows.start
    column = lax.broadcasted_iota(jnp.int32, shape, 1) + columns.start
    group = lax.shift_right_logical(row * 57, 9)
    inner = row - 9 * group
    upper = lax.shift_right_logical(inner * 11, 5)
    side = 2 * (face % 2)
    if face // 2 == 0:
        within = 9 * side + inner
    elif face // 2 == 1:
        within = 9 * upper + 3 * side + inner - 3 * upper
    else:
        within = 3 * inner + side
    hit = (column == 27 * group + within) & (row < NV * NODES)
    return jnp.where(hit, 1.0, 0.0).astype(jnp.bfloat16)


def trace_kernel(state_ref, trace_ref, *refs):
    head_refs = refs[:4]
    main_ref, late_ref = refs[4:]
    unknowns, count = state_ref.shape
    width = head_refs[0].shape[1]
    early = min(unknowns, WIDE)
    tail = late_rows(unknowns)
    rest = SLOT - tail
    for face in range(6):
        main_ref[face * SLOT : (face + 1) * SLOT, :] = picks(face, range(SLOT), range(early))
        late_ref[face * rest : (face + 1) * rest, :] = picks(face, range(tail, SLOT), range(early, unknowns))
    for chunk in range(count // WIDE):
        cols = slice(chunk * WIDE, (chunk + 1) * WIDE)
        main = dot(main_ref[...], state_ref[:early, cols])
        late = dot(late_ref[...], state_ref[early:, cols])
        for face in range(6):
            first = face * SLOT
            trace_ref[face, chunk, :tail, :] = main[first : first + tail].astype(jnp.bfloat16)
            both = main[first + tail : first + SLOT] + late[face * rest : (face + 1) * rest]
            trace_ref[face, chunk, tail:, :] = both.astype(jnp.bfloat16)
    for axis, which in enumerate(BOTH[::-1]):
        flip = odd(which)
        low, high = (trace_ref[2 * axis + side, 0, :, :width] for side in range(2))
        head_refs[2 * axis][...] = jnp.where(flip, low, high)
        head_refs[2 * axis + 1][...] = jnp.where(flip, high, low)


def late_rows(unknowns):
    rows = np.stack([face_rows(face) for face in range(6)])
    return int(np.nonzero((rows >= min(unknowns, WIDE)).any(axis=0))[0][0]) // 16 * 16


def all_traces(flow_state, head_count):
    unknowns, count = flow_state.shape
    early = min(unknowns, WIDE)
    shapes = [(6, count // WIDE, SLOT, WIDE)] + [(SLOT, head_count)] * 4
    return pl.pallas_call(
        trace_kernel,
        in_specs=[VMEM],
        out_specs=[VMEM] * 5,
        out_shape=[jax.ShapeDtypeStruct(shape, jnp.bfloat16) for shape in shapes],
        scratch_shapes=[
            pltpu.VMEM((6 * SLOT, early), jnp.bfloat16),
            pltpu.VMEM((6 * (SLOT - late_rows(unknowns)), unknowns - early), jnp.bfloat16),
        ],
        compiler_params=pltpu.CompilerParams(vmem_limit_bytes=24 << 20),
        cost_estimate=pl.CostEstimate(flops=1 << 30, bytes_accessed=4 << 20, transcendentals=0),
        name="all_traces",
    )(flow_state)


def chosen(index, rows):
    row = lax.broadcasted_iota(jnp.int32, (rows, index.shape[1]), 0)
    return jnp.where(row == index, 1.0, 0.0).astype(jnp.bfloat16)


def local_kernel(trace_ref, nbr_ref, volume_ref, lift_ref, jac_ref, left_ref, right_ref, same_ref, out_ref, weights_ref, flux_mat_ref):
    chunks = trace_ref.shape[1]
    spread = dot(left_ref[...], jac_ref[...]).astype(jnp.bfloat16)
    spread = dot(spread, right_ref[...])
    for face in range(6):
        both = spread[:, face * 2 * SLOT : (face + 1) * 2 * SLOT]
        flux_mat_ref[face] = (both * same_ref[...]).astype(jnp.bfloat16)
    unknowns = volume_ref.shape[1]
    values = lift_ref.shape[2]
    first, second, total_width = operand_places(unknowns)
    for direction in range(4):
        weights_ref[direction, :, :unknowns] = volume_ref[direction]
        weights_ref[direction, :, unknowns:] = jnp.zeros((unknowns, total_width - unknowns), jnp.bfloat16)
        if direction < 3:
            weights_ref[direction, :, first : first + values] = lift_ref[2 * direction]
            weights_ref[direction, :, second : second + values] = lift_ref[2 * direction + 1]
    for step in range(chunks):
        here = slice(step * WIDE, (step + 1) * WIDE)
        for face in range(6):
            index = nbr_ref[face : face + 1, here]
            part = lax.shift_right_logical(index, WIDE.bit_length() - 1)
            source = trace_ref[face ^ 1].reshape(chunks * SLOT, WIDE)
            each = dot(source, chosen(jnp.bitwise_and(index, WIDE - 1), WIDE))
            found = jnp.where(part == 0, each[:SLOT], 0.0)
            for chunk in range(1, chunks):
                found = jnp.where(part == chunk, each[chunk * SLOT : (chunk + 1) * SLOT], found)
            out_ref[face, :, here] = found.astype(jnp.bfloat16)


def operand_places(unknowns):
    first = -(-unknowns // 16) * 16
    second = -(-(first + SLOT) // 128) * 128
    return first, second, second + SLOT


def local_traces(traces, face_nbr, volume_ops, lift_ops, jac):
    faces, chunks, slot, wide = traces.shape
    unknowns = volume_ops.shape[1]
    args = (traces, face_nbr, volume_ops, lift_ops, jac, *kron_parts(12))
    return pl.pallas_call(
        local_kernel,
        in_specs=[VMEM] * len(args),
        out_specs=[VMEM] * 3,
        out_shape=[
            jax.ShapeDtypeStruct((faces, slot, chunks * wide), jnp.bfloat16),
            jax.ShapeDtypeStruct((4, unknowns, operand_places(unknowns)[2]), jnp.bfloat16),
            jax.ShapeDtypeStruct((6, SLOT, 2 * SLOT), jnp.bfloat16),
        ],
        compiler_params=pltpu.CompilerParams(vmem_limit_bytes=24 << 20),
        cost_estimate=pl.CostEstimate(flops=2 << 30, bytes_accessed=4 << 20, transcendentals=0),
        name="local_traces",
    )(*args)


def flow_kernel(directions, state_ref, nbr_ref, trace_ref, local_ref, weights_ref, flux_mat_ref, *refs):
    unknowns, count = state_ref.shape
    first, second, height = operand_places(unknowns)
    out_ref = refs[0]
    if len(refs) > 1:
        out_ref, remote_ref = refs[4:]
        for axis, which in enumerate(BOTH[::-1]):
            flip = odd(which)
            partner, other = refs[2 * axis][...], refs[2 * axis + 1][...]
            remote_ref[2 * axis] = jnp.where(flip, partner, other)
            remote_ref[2 * axis + 1] = jnp.where(flip, other, partner)
    faces = [2 * direction + side for direction in directions if direction < 3 for side in range(2)]

    def some(places):
        wheres = [slice(p * WIDE, (p + 1) * WIDE) for p in places]
        found = {}
        for here in wheres:
            for face in faces:
                found[here.start, face] = local_ref[face, :, here]
                if face < 4:
                    index = nbr_ref[face : face + 1, here] - count
                    remote = dot(remote_ref[face], chosen(index, remote_ref.shape[2]))
                    found[here.start, face] += remote.astype(jnp.bfloat16)
        fluxes = {}
        for p, here in zip(places, wheres):
            for face in faces:
                sides = jnp.concatenate([trace_ref[face, p], found[here.start, face]], axis=0)
                fluxes[p, face] = dot(flux_mat_ref[face], sides).astype(jnp.bfloat16)
        gap = jnp.zeros((second - first - SLOT, WIDE), jnp.bfloat16)
        for p, here in zip(places, wheres):
            own = state_ref[:, here]
            own_padded = jnp.concatenate([own, jnp.zeros((first - unknowns, WIDE), jnp.bfloat16)], axis=0)
            for place, direction in enumerate(directions):
                if direction < 3:
                    operand = [own_padded, fluxes[p, 2 * direction], gap, fluxes[p, 2 * direction + 1]]
                    out_ref[place, :, here] = dot(weights_ref[direction], jnp.concatenate(operand, axis=0))
                else:
                    out_ref[place, :, here] = dot(weights_ref[direction, :, :unknowns], own)

    chunks = count // WIDE
    for start in range(0, chunks, 2):
        some(range(start, min(start + 2, chunks)))


def flow_parts(directions, flow_state, face_nbr, traces, local, weights, flux_mat, *remotes):
    unknowns, count = flow_state.shape
    args = (flow_state, face_nbr, traces, local, weights, flux_mat, *remotes)
    return pl.pallas_call(
        functools.partial(flow_kernel, directions),
        in_specs=[VMEM] * len(args),
        out_specs=VMEM,
        out_shape=jax.ShapeDtypeStruct((len(directions), unknowns, count), jnp.float32),
        scratch_shapes=[pltpu.VMEM((4, *remotes[0].shape), jnp.bfloat16)] if remotes else [],
        compiler_params=pltpu.CompilerParams(vmem_limit_bytes=32 << 20),
        cost_estimate=pl.CostEstimate(flops=2 << 30, bytes_accessed=4 << 20, transcendentals=0),
        name="flow_parts",
    )(*args)


def total(tiles):
    tile = functools.reduce(jnp.add, tiles)
    tile = jnp.sum(jnp.sum(tile, axis=0, keepdims=True), axis=1, keepdims=True)
    return jnp.broadcast_to(tile, (TILE, 128))


def wall_kernel(
    masks, kind_bits, rows, own_rows,
    near_ref, far_ref, base_ref, follow_ref, anchor_ref, parts0_ref, parts1_ref, residual_ref, disp_ref,
    disp, resid, applied, search, image, diag,
):
    comps = 3
    tiles = rows // TILE
    me = lax.axis_index(BOTH)
    flip = kind(me, kind_bits) == 1

    def strided(block):
        first = block * TILE
        return pl.ds((first % tiles) * TILE + first // tiles, TILE, stride=TILE)

    each = 3 * comps * own_rows
    half = near_ref.shape[0] // each
    for pair in range(half):
        ref, at = (near_ref, pair) if pair < half // 2 else (far_ref, pair - half // 2)
        both = ref[2 * at * each : 2 * (at + 1) * each, :].astype(jnp.float32)
        for slot in range(2):
            device = jnp.bitwise_xor(me, jnp.where(flip, masks[1][2 * pair + slot], masks[0][2 * pair + slot]))
            upper, lower, stiff = (both[slot * each + k * comps * own_rows :][: comps * own_rows] for k in range(3))
            load = upper + lower
            for block in range(own_rows // TILE):
                to = strided(device * (own_rows // TILE) + block)
                for c in range(comps):
                    first = c * own_rows + block * TILE
                    resid[c, to, :] = load[first : first + TILE]
                    diag[c, to, :] = 4.0 + stiff[first : first + TILE]

    lane = lax.broadcasted_iota(jnp.int32, (TILE, 128), 1)
    sub = lax.broadcasted_iota(jnp.int32, (TILE, 128), 0)
    group = 32 if tiles % 32 == 0 else 8
    zero = jnp.zeros((TILE, 128), jnp.float32)

    def at(tile):
        return pl.ds(tile * TILE if isinstance(tile, int) else pl.multiple_of(tile * TILE, TILE), TILE)

    def sweep(renew):
        norms, energies = [], []
        for c in range(comps):
            above = jnp.where(sub == 0, 0.0, pltpu.roll(renew(c, tiles - 1, False), 1, 0))

            def operate(tile, above, value, below, c=c):
                beside = above + below
                beside += jnp.where(lane == 0, 0.0, pltpu.roll(value, 1, 1))
                beside += jnp.where(lane == 127, 0.0, pltpu.roll(value, 127, 1))
                result = diag[c, at(tile), :] * value - beside
                applied[c, at(tile), :] = result
                return value * value, value * result

            def some(chunk, carry, c=c):
                above, value, norm, energy = carry
                norm, energy = [norm, zero], [energy, zero]
                for k in range(group):
                    tile = chunk * group + k + 1
                    below = renew(c, tile, True)
                    terms = operate(tile - 1, above, value, below)
                    norm[k % 2] += terms[0]
                    energy[k % 2] += terms[1]
                    above, value = value, below
                return above, value, norm[0] + norm[1], energy[0] + energy[1]

            first = value = renew(c, 0, True)
            norm = energy = zero
            if tiles > group:
                above, value, norm, energy = lax.fori_loop(0, tiles // group - 1, some, (above, value, norm, energy))
            norm, energy = [norm, zero], [energy, zero]
            for tile in range(tiles - group + 1, tiles + 1):
                if tile < tiles:
                    below = renew(c, tile, True)
                else:
                    below = jnp.where(sub == TILE - 1, 0.0, pltpu.roll(first, TILE - 1, 0))
                terms = operate(tile - 1, above, value, below)
                norm[tile % 2] += terms[0]
                energy[tile % 2] += terms[1]
                above, value = value, below
            norms += norm
            energies += energy
        return total(norms), total(energies)

    def begin(c, tile, keep):
        return resid[c, at(tile), :]

    def advance(step_size, ratio, last_step=None, first=False):
        def renew(c, tile, keep):
            value = resid[c, at(tile), :]
            toward, moved = value, applied[c, at(tile), :]
            if not first:
                before = search[c, at(tile), :]
                toward += ratio * before
                moved += ratio * image[c, at(tile), :]
            value -= step_size * moved
            if keep:
                search[c, at(tile), :] = toward
                image[c, at(tile), :] = moved
                resid[c, at(tile), :] = value
                if last_step is not None:
                    disp[c, at(tile), :] += last_step * before + step_size * toward
            return value

        return renew

    def sizes(norm, energy, last_norm, last_curve):
        ratio = norm / last_norm
        curve = energy - ratio * ratio * last_curve
        return norm / curve, ratio, curve

    norm, curve = sweep(begin)
    step_size = norm / curve
    last_norm, last_curve, last_step = norm, curve, step_size
    norm, energy = sweep(advance(step_size, None, first=True))

    def clear(tile, carry):
        for c in range(comps):
            disp[c, at(tile), :] = zero
        return carry

    lax.fori_loop(0, tiles, clear, 0, unroll=8)

    def two(position, carry):
        norm, energy, last_norm, last_curve, last_step = carry
        step_size, ratio, curve = sizes(norm, energy, last_norm, last_curve)
        last_norm = norm
        norm, energy = sweep(advance(step_size, ratio, last_step))
        step_size, ratio, curve = sizes(norm, energy, last_norm, curve)
        last_norm = norm
        norm, energy = sweep(advance(step_size, ratio))
        return norm, energy, last_norm, curve, step_size

    assert ITERS % 2 == 0
    carry = lax.fori_loop(0, ITERS // 2 - 1, two, (norm, energy, last_norm, last_curve, last_step))
    norm, energy, last_norm, last_curve, last_step = carry
    step_size, ratio, curve = sizes(norm, energy, last_norm, last_curve)

    def finish(tile, carry):
        for c in range(comps):
            before = search[c, at(tile), :]
            toward = resid[c, at(tile), :] + ratio * before
            disp[c, at(tile), :] += last_step * before + step_size * toward
        return carry

    lax.fori_loop(0, tiles, finish, 0, unroll=8)

    for block in range(own_rows // TILE):
        for c in range(comps):
            disp_ref[c, block * TILE : (block + 1) * TILE, :] = disp[c, strided(me * (own_rows // TILE) + block), :]

    anchor = anchor_ref[...]
    count = anchor.shape[1]
    row = anchor // 128
    column = anchor - row * 128
    upper = row // tiles
    place = (row - upper * tiles) * TILE + upper
    some_rows = 128
    run = lax.shift_right_logical(place, 7)
    pair = lax.shift_right_logical(run, 1)
    inner = place - some_rows * run
    pick = chosen(column + 128 * (run - 2 * pair), 256)
    pick = jnp.concatenate([pick, pick], axis=0)
    row_of = lax.broadcasted_iota(jnp.int32, (some_rows, count), 0)

    def look(chunk, sums):
        hit = row_of == jnp.where(pair == chunk, inner, -1)
        out = []
        for c in range(comps):
            values = [disp[c, pl.ds(pl.multiple_of((2 * chunk + k) * some_rows, some_rows), some_rows), :] for k in range(2)]
            value = jnp.concatenate(values, axis=1)
            coarse = value.astype(jnp.bfloat16)
            fine = (value - coarse.astype(jnp.float32)).astype(jnp.bfloat16)
            found = dot(jnp.concatenate([coarse, fine], axis=1), pick)
            found = jnp.where(hit, found, 0.0).reshape(some_rows // TILE, TILE, count)
            out.append(sums[c] + jnp.sum(found, axis=0))
        return tuple(out)

    sums = (jnp.zeros((TILE, count), jnp.float32),) * comps
    chunks = rows // (2 * some_rows)
    sums = lax.fori_loop(0, chunks, look, sums, unroll=chunks <= 2)
    follow = follow_ref[...]
    geometry = [
        base_ref[c : c + 1, :] * jnp.exp(follow * jnp.sum(sums[c], axis=0, keepdims=True)) for c in range(comps)
    ]
    geometry.append(base_ref[comps : comps + 1, :])
    unknowns = residual_ref.shape[0]
    parts = [(ref, place) for ref in (parts0_ref, parts1_ref) for place in range(ref.shape[0])]
    for first in range(0, unknowns, 16):
        some = slice(first, min(first + 16, unknowns))
        terms = [factor * ref[place, some, :] for factor, (ref, place) in zip(geometry, parts)]
        residual_ref[some, :] = functools.reduce(jnp.add, terms).astype(jnp.bfloat16)


def wall_and_residual(near, far, masks, kind_bits, base_geometry, anchor_weight, wall_anchor, parts, own_rows):
    rows = own_rows * len(masks[0])
    unknowns, count = parts[0].shape[1], anchor_weight.shape[0]
    field = pltpu.VMEM((3, rows, 128), jnp.float32)
    return pl.pallas_call(
        functools.partial(wall_kernel, masks, kind_bits, rows, own_rows),
        in_specs=[VMEM] * 7,
        out_specs=[VMEM] * 2,
        out_shape=[
            jax.ShapeDtypeStruct((unknowns, count), jnp.bfloat16),
            jax.ShapeDtypeStruct((3, own_rows, 128), jnp.float32),
        ],
        scratch_shapes=[
            field,
            field,
            field,
            field,
            field,
            field,
        ],
        compiler_params=pltpu.CompilerParams(vmem_limit_bytes=(16 << 20) + 16 * rows * 3 * 128 * 4),
        cost_estimate=pl.CostEstimate(flops=4 << 30, bytes_accessed=8 << 20, transcendentals=0),
        name="wall_and_residual",
    )(near, far, base_geometry, anchor_weight[None, :], wall_anchor[None, :], *parts)


def paired(x, axis, offset):
    peers = lax.axis_size(axis)
    pairs = [((i + offset) % peers, (i + offset + 1) % peers) for i in range(0, peers, 2)]
    return lax.ppermute(x, axis, pairs + [pair[::-1] for pair in pairs])


def gather_stages(mesh):
    n_sec, n_dom = mesh.shape["sec"], mesh.shape["dom"]
    assert n_sec & (n_sec - 1) == 0 and n_dom & (n_dom - 1) == 0 and n_sec > 1
    bits = [1 << b for b in range((n_sec * n_dom).bit_length() - 1)]
    inner, outer = bits[: n_dom.bit_length() - 1], bits[n_dom.bit_length() :]
    order = inner[::-1] + outer[::-1]
    first = [bit ^ n_dom for bit in order]
    second = first[:-2] + first[-2:][::-1]
    return (first + [n_dom], second + [n_dom]), order[-2:] + [n_dom]


def kind(device, bits):
    return sum(device // bit % 2 for bit in bits) % 2


def on_device(
    stages, kind_bits,
    flow_state, base_geometry, anchor_weight, wall_anchor, face_nbr, volume_ops, lift_ops, face_jac, wall_load, wall_stiff,
):
    own_rows, width = wall_load.shape[1:]
    wall = jnp.concatenate([wall_load, wall_load, wall_stiff], axis=0).reshape(9 * own_rows, width)
    third = lax.broadcasted_iota(jnp.int32, wall.shape, 0) // (3 * own_rows)
    wall = jnp.where(third == 1, wall - lax.reduce_precision(wall, 8, 7), wall).astype(jnp.bfloat16)
    masks = []
    for bits in stages:
        masks.append([0])
        for bit in bits[:-1]:
            masks[-1] += [m ^ bit for m in masks[-1]]
    masks = [ours + [m ^ stages[0][-1] for m in theirs] for ours, theirs in (masks, masks[::-1])]
    devices = lax.axis_size(BOTH)

    def sent(wall, position):
        pairs = [(i, i ^ stages[kind(i, kind_bits)][position]) for i in range(devices)]
        return lax.ppermute(wall, BOTH, pairs)

    barrier = lax.optimization_barrier
    far = sent(wall, 0)
    head_count = flow_state.shape[1] // 8
    traces, *heads = all_traces(flow_state, head_count)
    remotes = [None] * 4
    far, heads = barrier((far, heads))
    wall = jnp.concatenate([wall, far], axis=0)
    far = sent(wall, 1)
    remotes[1] = paired(heads[1], "dom", 1)
    far, heads, face_jac = barrier((far, heads, face_jac))
    wall = jnp.concatenate([wall, far], axis=0)
    far = sent(wall, 2)
    jac = face_jac.transpose(2, 0, 1, 3).reshape(NV, 12 * NV)
    remotes[2] = paired(heads[2], "sec", 0)
    remotes[0] = paired(heads[0], "dom", 0)
    remotes[3] = paired(heads[3], "sec", 1)
    far, traces, volume_ops, jac, remotes[1] = barrier((far, traces, volume_ops, jac, remotes[1]))
    wall = jnp.concatenate([wall, far], axis=0)
    far = sent(wall, 3)
    local, weights, flux_mat = local_traces(traces, face_nbr, volume_ops, lift_ops, jac)
    common = (flow_state, face_nbr, traces, local, weights, flux_mat)
    inner = flow_parts((2, 3), *common)
    far, inner, remotes[0], remotes[2], remotes[3] = barrier((far, inner, remotes[0], remotes[2], remotes[3]))
    for position in range(4, len(stages[0])):
        wall = jnp.concatenate([wall, far], axis=0)
        far = sent(wall, position)
    outer = flow_parts((0, 1), *common, *remotes)
    halves = (outer, inner)
    return wall_and_residual(wall, far, masks, kind_bits, base_geometry, anchor_weight, wall_anchor, halves, own_rows)


def solution(mesh):
    return jax.shard_map(
        functools.partial(on_device, *gather_stages(mesh)),
        mesh=mesh,
        in_specs=(
            P(None, BOTH),
            P(None, BOTH),
            P(BOTH),
            P(BOTH),
            P(None, BOTH),
            P(),
            P(),
            P(),
            P(None, BOTH, None),
            P(None, BOTH, None),
        ),
        out_specs=(P(None, BOTH), P(None, BOTH, None)),
        check_vma=False,
    )
```

```python
import functools

import jax
import jax.numpy as jnp
import numpy as np
from jax import lax
from jax.experimental import pallas as pl
from jax.experimental.pallas import tpu as pltpu
from jax.sharding import PartitionSpec as P

NV = 5
ITERS = 8
NODES = 18
SLOT = 96
TILE = 8
WIDE = 256
BOTH = ("sec", "dom")


def face_rows(face):
    rows = np.arange(NV * 54).reshape(NV * 2, 3, 3, 3)
    return np.take(rows, 0 if face % 2 == 0 else 2, axis=1 + face // 2).reshape(-1)


def kron_parts(sides):
    row = np.arange(SLOT)
    valid = row < NV * NODES
    variable, node = row // NODES, row % NODES
    left = np.zeros((SLOT, NV), np.float32)
    left[row[valid], variable[valid]] = 1
    right = np.zeros((sides * NV, sides * SLOT), np.float32)
    for side in range(sides):
        right[side * NV + variable[valid], side * SLOT + row[valid]] = 1
    same = (node[:, None] == node[None, :]) & valid[:, None] & valid[None, :]
    return (
        jnp.asarray(left, jnp.bfloat16),
        jnp.asarray(right, jnp.bfloat16),
        jnp.asarray(np.concatenate([same, same], axis=1), jnp.float32),
    )


def dot(a, b):
    return jnp.dot(a, b, preferred_element_type=jnp.float32)


VMEM = pl.BlockSpec(memory_space=pltpu.VMEM)

HBM = pl.BlockSpec(memory_space=pltpu.HBM)


def odd(axis):
    return lax.rem(lax.axis_index(axis), 2) == 1


def picks(face, rows, columns):
    shape = (rows.stop - rows.start, columns.stop - columns.start)
    row = lax.broadcasted_iota(jnp.int32, shape, 0) + rows.start
    column = lax.broadcasted_iota(jnp.int32, shape, 1) + columns.start
    group = lax.shift_right_logical(row * 57, 9)
    inner = row - 9 * group
    upper = lax.shift_right_logical(inner * 11, 5)
    side = 2 * (face % 2)
    if face // 2 == 0:
        within = 9 * side + inner
    elif face // 2 == 1:
        within = 9 * upper + 3 * side + inner - 3 * upper
    else:
        within = 3 * inner + side
    hit = (column == 27 * group + within) & (row < NV * NODES)
    return jnp.where(hit, 1.0, 0.0).astype(jnp.bfloat16)


def trace_kernel(state_ref, trace_ref, *refs):
    head_refs = refs[:4]
    main_ref, late_ref = refs[4:]
    unknowns, count = state_ref.shape
    width = head_refs[0].shape[1]
    early = min(unknowns, WIDE)
    tail = late_rows(unknowns)
    rest = SLOT - tail
    for face in range(6):
        main_ref[face * SLOT : (face + 1) * SLOT, :] = picks(face, range(SLOT), range(early))
        late_ref[face * rest : (face + 1) * rest, :] = picks(face, range(tail, SLOT), range(early, unknowns))
    for chunk in range(count // WIDE):
        cols = slice(chunk * WIDE, (chunk + 1) * WIDE)
        main = dot(main_ref[...], state_ref[:early, cols])
        late = dot(late_ref[...], state_ref[early:, cols])
        for face in range(6):
            first = face * SLOT
            trace_ref[face, chunk, :tail, :] = main[first : first + tail].astype(jnp.bfloat16)
            both = main[first + tail : first + SLOT] + late[face * rest : (face + 1) * rest]
            trace_ref[face, chunk, tail:, :] = both.astype(jnp.bfloat16)
    for axis, which in enumerate(BOTH[::-1]):
        flip = odd(which)
        low, high = (trace_ref[2 * axis + side, 0, :, :width] for side in range(2))
        head_refs[2 * axis][...] = jnp.where(flip, low, high)
        head_refs[2 * axis + 1][...] = jnp.where(flip, high, low)


def late_rows(unknowns):
    rows = np.stack([face_rows(face) for face in range(6)])
    return int(np.nonzero((rows >= min(unknowns, WIDE)).any(axis=0))[0][0]) // 16 * 16


def all_traces(flow_state, head_count):
    unknowns, count = flow_state.shape
    early = min(unknowns, WIDE)
    shapes = [(6, count // WIDE, SLOT, WIDE)] + [(SLOT, head_count)] * 4
    return pl.pallas_call(
        trace_kernel,
        in_specs=[VMEM],
        out_specs=[VMEM] * 5,
        out_shape=[jax.ShapeDtypeStruct(shape, jnp.bfloat16) for shape in shapes],
        scratch_shapes=[
            pltpu.VMEM((6 * SLOT, early), jnp.bfloat16),
            pltpu.VMEM((6 * (SLOT - late_rows(unknowns)), unknowns - early), jnp.bfloat16),
        ],
        compiler_params=pltpu.CompilerParams(vmem_limit_bytes=24 << 20),
        cost_estimate=pl.CostEstimate(flops=1 << 30, bytes_accessed=4 << 20, transcendentals=0),
        name="all_traces",
    )(flow_state)


def chosen(index, rows):
    row = lax.broadcasted_iota(jnp.int32, (rows, index.shape[1]), 0)
    return jnp.where(row == index, 1.0, 0.0).astype(jnp.bfloat16)


def local_kernel(trace_ref, nbr_ref, volume_ref, lift_ref, jac_ref, left_ref, right_ref, same_ref, out_ref, weights_ref, flux_mat_ref):
    chunks = trace_ref.shape[1]
    spread = dot(left_ref[...], jac_ref[...]).astype(jnp.bfloat16)
    spread = dot(spread, right_ref[...])
    for face in range(6):
        both = spread[:, face * 2 * SLOT : (face + 1) * 2 * SLOT]
        flux_mat_ref[face] = (both * same_ref[...]).astype(jnp.bfloat16)
    unknowns = volume_ref.shape[1]
    values = lift_ref.shape[2]
    first, second, total_width = operand_places(unknowns)
    for direction in range(4):
        weights_ref[direction, :, :unknowns] = volume_ref[direction]
        weights_ref[direction, :, unknowns:] = jnp.zeros((unknowns, total_width - unknowns), jnp.bfloat16)
        if direction < 3:
            weights_ref[direction, :, first : first + values] = lift_ref[2 * direction]
            weights_ref[direction, :, second : second + values] = lift_ref[2 * direction + 1]
    for step in range(chunks):
        here = slice(step * WIDE, (step + 1) * WIDE)
        for face in range(6):
            index = nbr_ref[face : face + 1, here]
            part = lax.shift_right_logical(index, WIDE.bit_length() - 1)
            source = trace_ref[face ^ 1].reshape(chunks * SLOT, WIDE)
            each = dot(source, chosen(jnp.bitwise_and(index, WIDE - 1), WIDE))
            found = jnp.where(part == 0, each[:SLOT], 0.0)
            for chunk in range(1, chunks):
                found = jnp.where(part == chunk, each[chunk * SLOT : (chunk + 1) * SLOT], found)
            out_ref[face, :, here] = found.astype(jnp.bfloat16)


def operand_places(unknowns):
    first = -(-unknowns // 16) * 16
    second = -(-(first + SLOT) // 128) * 128
    return first, second, second + SLOT


def local_traces(traces, face_nbr, volume_ops, lift_ops, jac):
    faces, chunks, slot, wide = traces.shape
    unknowns = volume_ops.shape[1]
    args = (traces, face_nbr, volume_ops, lift_ops, jac, *kron_parts(12))
    return pl.pallas_call(
        local_kernel,
        in_specs=[VMEM] * len(args),
        out_specs=[VMEM] * 3,
        out_shape=[
            jax.ShapeDtypeStruct((faces, slot, chunks * wide), jnp.bfloat16),
            jax.ShapeDtypeStruct((4, unknowns, operand_places(unknowns)[2]), jnp.bfloat16),
            jax.ShapeDtypeStruct((6, SLOT, 2 * SLOT), jnp.bfloat16),
        ],
        compiler_params=pltpu.CompilerParams(vmem_limit_bytes=24 << 20),
        cost_estimate=pl.CostEstimate(flops=2 << 30, bytes_accessed=4 << 20, transcendentals=0),
        name="local_traces",
    )(*args)


def flow_kernel(directions, state_ref, nbr_ref, trace_ref, local_ref, weights_ref, flux_mat_ref, *refs):
    unknowns, count = state_ref.shape
    first, second, height = operand_places(unknowns)
    out_ref = refs[0]
    if len(refs) > 1:
        out_ref, remote_ref = refs[4:]
        for axis, which in enumerate(BOTH[::-1]):
            flip = odd(which)
            partner, other = refs[2 * axis][...], refs[2 * axis + 1][...]
            remote_ref[2 * axis] = jnp.where(flip, partner, other)
            remote_ref[2 * axis + 1] = jnp.where(flip, other, partner)
    faces = [2 * direction + side for direction in directions if direction < 3 for side in range(2)]

    def some(places):
        wheres = [slice(p * WIDE, (p + 1) * WIDE) for p in places]
        found = {}
        for here in wheres:
            for face in faces:
                found[here.start, face] = local_ref[face, :, here]
                if face < 4:
                    index = nbr_ref[face : face + 1, here] - count
                    remote = dot(remote_ref[face], chosen(index, remote_ref.shape[2]))
                    found[here.start, face] += remote.astype(jnp.bfloat16)
        fluxes = {}
        for p, here in zip(places, wheres):
            for face in faces:
                sides = jnp.concatenate([trace_ref[face, p], found[here.start, face]], axis=0)
                fluxes[p, face] = dot(flux_mat_ref[face], sides).astype(jnp.bfloat16)
        gap = jnp.zeros((second - first - SLOT, WIDE), jnp.bfloat16)
        for p, here in zip(places, wheres):
            own = state_ref[:, here]
            own_padded = jnp.concatenate([own, jnp.zeros((first - unknowns, WIDE), jnp.bfloat16)], axis=0)
            for place, direction in enumerate(directions):
                if direction < 3:
                    operand = [own_padded, fluxes[p, 2 * direction], gap, fluxes[p, 2 * direction + 1]]
                    out_ref[place, :, here] = dot(weights_ref[direction], jnp.concatenate(operand, axis=0))
                else:
                    out_ref[place, :, here] = dot(weights_ref[direction, :, :unknowns], own)

    chunks = count // WIDE
    for start in range(0, chunks, 2):
        some(range(start, min(start + 2, chunks)))


def flow_parts(directions, flow_state, face_nbr, traces, local, weights, flux_mat, *remotes):
    unknowns, count = flow_state.shape
    args = (flow_state, face_nbr, traces, local, weights, flux_mat, *remotes)
    return pl.pallas_call(
        functools.partial(flow_kernel, directions),
        in_specs=[VMEM] * len(args),
        out_specs=VMEM,
        out_shape=jax.ShapeDtypeStruct((len(directions), unknowns, count), jnp.float32),
        scratch_shapes=[pltpu.VMEM((4, *remotes[0].shape), jnp.bfloat16)] if remotes else [],
        compiler_params=pltpu.CompilerParams(vmem_limit_bytes=32 << 20),
        cost_estimate=pl.CostEstimate(flops=2 << 30, bytes_accessed=4 << 20, transcendentals=0),
        name="flow_parts",
    )(*args)


def total(tiles):
    tile = functools.reduce(jnp.add, tiles)
    tile = jnp.sum(jnp.sum(tile, axis=0, keepdims=True), axis=1, keepdims=True)
    return jnp.broadcast_to(tile, (TILE, 128))


def wall_kernel(
    masks, kind_bits, rows, own_rows,
    near_ref, far_ref, base_ref, follow_ref, anchor_ref, parts0_ref, parts1_ref, residual_ref, disp_ref,
    disp, resid, applied, search, image, diag,
):
    comps = 3
    tiles = rows // TILE
    me = lax.axis_index(BOTH)
    flip = kind(me, kind_bits) == 1

    def strided(block):
        first = block * TILE
        return pl.ds((first % tiles) * TILE + first // tiles, TILE, stride=TILE)

    each = 3 * comps * own_rows
    half = near_ref.shape[0] // each
    for pair in range(half):
        ref, at = (near_ref, pair) if pair < half // 2 else (far_ref, pair - half // 2)
        both = ref[2 * at * each : 2 * (at + 1) * each, :].astype(jnp.float32)
        for slot in range(2):
            device = jnp.bitwise_xor(me, jnp.where(flip, masks[1][2 * pair + slot], masks[0][2 * pair + slot]))
            upper, lower, stiff = (both[slot * each + k * comps * own_rows :][: comps * own_rows] for k in range(3))
            load = upper + lower
            for block in range(own_rows // TILE):
                to = strided(device * (own_rows // TILE) + block)
                for c in range(comps):
                    first = c * own_rows + block * TILE
                    resid[c, to, :] = load[first : first + TILE]
                    diag[c, to, :] = 4.0 + stiff[first : first + TILE]

    lane = lax.broadcasted_iota(jnp.int32, (TILE, 128), 1)
    sub = lax.broadcasted_iota(jnp.int32, (TILE, 128), 0)
    group = 32 if tiles % 32 == 0 else 8
    zero = jnp.zeros((TILE, 128), jnp.float32)

    def at(tile):
        return pl.ds(tile * TILE if isinstance(tile, int) else pl.multiple_of(tile * TILE, TILE), TILE)

    def sweep(renew):
        norms, energies = [], []
        for c in range(comps):
            above = jnp.where(sub == 0, 0.0, pltpu.roll(renew(c, tiles - 1, False), 1, 0))

            def operate(tile, above, value, below, c=c):
                beside = above + below
                beside += jnp.where(lane == 0, 0.0, pltpu.roll(value, 1, 1))
                beside += jnp.where(lane == 127, 0.0, pltpu.roll(value, 127, 1))
                result = diag[c, at(tile), :] * value - beside
                applied[c, at(tile), :] = result
                return value * value, value * result

            def some(chunk, carry, c=c):
                above, value, norm, energy = carry
                norm, energy = [norm, zero], [energy, zero]
                for k in range(group):
                    tile = chunk * group + k + 1
                    below = renew(c, tile, True)
                    terms = operate(tile - 1, above, value, below)
                    norm[k % 2] += terms[0]
                    energy[k % 2] += terms[1]
                    above, value = value, below
                return above, value, norm[0] + norm[1], energy[0] + energy[1]

            first = value = renew(c, 0, True)
            norm = energy = zero
            if tiles > group:
                above, value, norm, energy = lax.fori_loop(0, tiles // group - 1, some, (above, value, norm, energy))
            norm, energy = [norm, zero], [energy, zero]
            for tile in range(tiles - group + 1, tiles + 1):
                if tile < tiles:
                    below = renew(c, tile, True)
                else:
                    below = jnp.where(sub == TILE - 1, 0.0, pltpu.roll(first, TILE - 1, 0))
                terms = operate(tile - 1, above, value, below)
                norm[tile % 2] += terms[0]
                energy[tile % 2] += terms[1]
                above, value = value, below
            norms += norm
            energies += energy
        return total(norms), total(energies)

    def begin(c, tile, keep):
        return resid[c, at(tile), :]

    def advance(step_size, ratio, last_step=None, first=False):
        def renew(c, tile, keep):
            value = resid[c, at(tile), :]
            toward, moved = value, applied[c, at(tile), :]
            if not first:
                before = search[c, at(tile), :]
                toward += ratio * before
                moved += ratio * image[c, at(tile), :]
            value -= step_size * moved
            if keep:
                search[c, at(tile), :] = toward
                image[c, at(tile), :] = moved
                resid[c, at(tile), :] = value
                if last_step is not None:
                    disp[c, at(tile), :] += last_step * before + step_size * toward
            return value

        return renew

    def sizes(norm, energy, last_norm, last_curve):
        ratio = norm / last_norm
        curve = energy - ratio * ratio * last_curve
        return norm / curve, ratio, curve

    norm, curve = sweep(begin)
    step_size = norm / curve
    last_norm, last_curve, last_step = norm, curve, step_size
    norm, energy = sweep(advance(step_size, None, first=True))

    def clear(tile, carry):
        for c in range(comps):
            disp[c, at(tile), :] = zero
        return carry

    lax.fori_loop(0, tiles, clear, 0, unroll=8)

    def two(position, carry):
        norm, energy, last_norm, last_curve, last_step = carry
        step_size, ratio, curve = sizes(norm, energy, last_norm, last_curve)
        last_norm = norm
        norm, energy = sweep(advance(step_size, ratio, last_step))
        step_size, ratio, curve = sizes(norm, energy, last_norm, curve)
        last_norm = norm
        norm, energy = sweep(advance(step_size, ratio))
        return norm, energy, last_norm, curve, step_size

    assert ITERS % 2 == 0
    carry = lax.fori_loop(0, ITERS // 2 - 1, two, (norm, energy, last_norm, last_curve, last_step))
    norm, energy, last_norm, last_curve, last_step = carry
    step_size, ratio, curve = sizes(norm, energy, last_norm, last_curve)

    def finish(tile, carry):
        for c in range(comps):
            before = search[c, at(tile), :]
            toward = resid[c, at(tile), :] + ratio * before
            disp[c, at(tile), :] += last_step * before + step_size * toward
        return carry

    lax.fori_loop(0, tiles, finish, 0, unroll=8)

    for block in range(own_rows // TILE):
        for c in range(comps):
            disp_ref[c, block * TILE : (block + 1) * TILE, :] = disp[c, strided(me * (own_rows // TILE) + block), :]

    anchor = anchor_ref[...]
    count = anchor.shape[1]
    row = anchor // 128
    column = anchor - row * 128
    upper = row // tiles
    place = (row - upper * tiles) * TILE + upper
    some_rows = 128
    run = lax.shift_right_logical(place, 7)
    pair = lax.shift_right_logical(run, 1)
    inner = place - some_rows * run
    pick = chosen(column + 128 * (run - 2 * pair), 256)
    pick = jnp.concatenate([pick, pick], axis=0)
    row_of = lax.broadcasted_iota(jnp.int32, (some_rows, count), 0)

    def look(chunk, sums):
        hit = row_of == jnp.where(pair == chunk, inner, -1)
        out = []
        for c in range(comps):
            values = [disp[c, pl.ds(pl.multiple_of((2 * chunk + k) * some_rows, some_rows), some_rows), :] for k in range(2)]
            value = jnp.concatenate(values, axis=1)
            coarse = value.astype(jnp.bfloat16)
            fine = (value - coarse.astype(jnp.float32)).astype(jnp.bfloat16)
            found = dot(jnp.concatenate([coarse, fine], axis=1), pick)
            found = jnp.where(hit, found, 0.0).reshape(some_rows // TILE, TILE, count)
            out.append(sums[c] + jnp.sum(found, axis=0))
        return tuple(out)

    sums = (jnp.zeros((TILE, count), jnp.float32),) * comps
    chunks = rows // (2 * some_rows)
    sums = lax.fori_loop(0, chunks, look, sums, unroll=chunks <= 2)
    follow = follow_ref[...]
    geometry = [
        base_ref[c : c + 1, :] * jnp.exp(follow * jnp.sum(sums[c], axis=0, keepdims=True)) for c in range(comps)
    ]
    geometry.append(base_ref[comps : comps + 1, :])
    unknowns = residual_ref.shape[0]
    parts = [(ref, place) for ref in (parts0_ref, parts1_ref) for place in range(ref.shape[0])]
    for first in range(0, unknowns, 16):
        some = slice(first, min(first + 16, unknowns))
        terms = [factor * ref[place, some, :] for factor, (ref, place) in zip(geometry, parts)]
        residual_ref[some, :] = functools.reduce(jnp.add, terms).astype(jnp.bfloat16)


def wall_and_residual(near, far, masks, kind_bits, base_geometry, anchor_weight, wall_anchor, parts, own_rows):
    rows = own_rows * len(masks[0])
    unknowns, count = parts[0].shape[1], anchor_weight.shape[0]
    field = pltpu.VMEM((3, rows, 128), jnp.float32)
    return pl.pallas_call(
        functools.partial(wall_kernel, masks, kind_bits, rows, own_rows),
        in_specs=[VMEM] * 7,
        out_specs=[VMEM] * 2,
        out_shape=[
            jax.ShapeDtypeStruct((unknowns, count), jnp.bfloat16),
            jax.ShapeDtypeStruct((3, own_rows, 128), jnp.float32),
        ],
        scratch_shapes=[
            field,
            field,
            field,
            field,
            field,
            field,
        ],
        compiler_params=pltpu.CompilerParams(vmem_limit_bytes=(16 << 20) + 16 * rows * 3 * 128 * 4),
        cost_estimate=pl.CostEstimate(flops=4 << 30, bytes_accessed=8 << 20, transcendentals=0),
        name="wall_and_residual",
    )(near, far, base_geometry, anchor_weight[None, :], wall_anchor[None, :], *parts)


def paired(x, axis, offset):
    peers = lax.axis_size(axis)
    pairs = [((i + offset) % peers, (i + offset + 1) % peers) for i in range(0, peers, 2)]
    return lax.ppermute(x, axis, pairs + [pair[::-1] for pair in pairs])


def gather_stages(mesh):
    n_sec, n_dom = mesh.shape["sec"], mesh.shape["dom"]
    assert n_sec & (n_sec - 1) == 0 and n_dom & (n_dom - 1) == 0 and n_sec > 1
    bits = [1 << b for b in range((n_sec * n_dom).bit_length() - 1)]
    inner, outer = bits[: n_dom.bit_length() - 1], bits[n_dom.bit_length() :]
    order = inner[::-1] + outer[::-1]
    order[:2] = order[1::-1]
    first = [bit ^ n_dom for bit in order]
    second = first[:-2] + first[-2:][::-1]
    return (first + [n_dom], second + [n_dom]), order[-2:] + [n_dom]


def kind(device, bits):
    return sum(device // bit % 2 for bit in bits) % 2


def on_device(
    stages, kind_bits,
    flow_state, base_geometry, anchor_weight, wall_anchor, face_nbr, volume_ops, lift_ops, face_jac, wall_load, wall_stiff,
):
    own_rows, width = wall_load.shape[1:]
    wall = jnp.concatenate([wall_load, wall_load, wall_stiff], axis=0).reshape(9 * own_rows, width)
    third = lax.broadcasted_iota(jnp.int32, wall.shape, 0) // (3 * own_rows)
    wall = jnp.where(third == 1, wall - lax.reduce_precision(wall, 8, 7), wall).astype(jnp.bfloat16)
    masks = []
    for bits in stages:
        masks.append([0])
        for bit in bits[:-1]:
            masks[-1] += [m ^ bit for m in masks[-1]]
    masks = [ours + [m ^ stages[0][-1] for m in theirs] for ours, theirs in (masks, masks[::-1])]
    devices = lax.axis_size(BOTH)

    def sent(wall, position):
        pairs = [(i, i ^ stages[kind(i, kind_bits)][position]) for i in range(devices)]
        return lax.ppermute(wall, BOTH, pairs)

    barrier = lax.optimization_barrier
    far = sent(wall, 0)
    head_count = flow_state.shape[1] // 8
    traces, *heads = all_traces(flow_state, head_count)
    remotes = [None] * 4
    far, heads = barrier((far, heads))
    wall = jnp.concatenate([wall, far], axis=0)
    far = sent(wall, 1)
    remotes[1] = paired(heads[1], "dom", 1)
    far, heads, face_jac = barrier((far, heads, face_jac))
    wall = jnp.concatenate([wall, far], axis=0)
    far = sent(wall, 2)
    jac = face_jac.transpose(2, 0, 1, 3).reshape(NV, 12 * NV)
    remotes[2] = paired(heads[2], "sec", 0)
    remotes[0] = paired(heads[0], "dom", 0)
    remotes[3] = paired(heads[3], "sec", 1)
    far, traces, volume_ops, jac, remotes[1] = barrier((far, traces, volume_ops, jac, remotes[1]))
    wall = jnp.concatenate([wall, far], axis=0)
    far = sent(wall, 3)
    local, weights, flux_mat = local_traces(traces, face_nbr, volume_ops, lift_ops, jac)
    common = (flow_state, face_nbr, traces, local, weights, flux_mat)
    inner = flow_parts((2, 3), *common)
    far, inner, remotes[0], remotes[2], remotes[3] = barrier((far, inner, remotes[0], remotes[2], remotes[3]))
    for position in range(4, len(stages[0])):
        wall = jnp.concatenate([wall, far], axis=0)
        far = sent(wall, position)
    outer = flow_parts((0, 1), *common, *remotes)
    halves = (outer, inner)
    return wall_and_residual(wall, far, masks, kind_bits, base_geometry, anchor_weight, wall_anchor, halves, own_rows)


def solution(mesh):
    return jax.shard_map(
        functools.partial(on_device, *gather_stages(mesh)),
        mesh=mesh,
        in_specs=(
            P(None, BOTH),
            P(None, BOTH),
            P(BOTH),
            P(BOTH),
            P(None, BOTH),
            P(),
            P(),
            P(),
            P(None, BOTH, None),
            P(None, BOTH, None),
        ),
        out_specs=(P(None, BOTH), P(None, BOTH, None)),
        check_vma=False,
    )
```

```python
import functools

import jax
import jax.numpy as jnp
import numpy as np
from jax import lax
from jax.experimental import pallas as pl
from jax.experimental.pallas import tpu as pltpu
from jax.sharding import PartitionSpec as P

NV = 5
ITERS = 8
NODES = 18
SLOT = 96
TILE = 8
WIDE = 256
BOTH = ("sec", "dom")


def face_rows(face):
    rows = np.arange(NV * 54).reshape(NV * 2, 3, 3, 3)
    return np.take(rows, 0 if face % 2 == 0 else 2, axis=1 + face // 2).reshape(-1)


def kron_parts(sides):
    row = np.arange(SLOT)
    valid = row < NV * NODES
    variable, node = row // NODES, row % NODES
    left = np.zeros((SLOT, NV), np.float32)
    left[row[valid], variable[valid]] = 1
    right = np.zeros((sides * NV, sides * SLOT), np.float32)
    for side in range(sides):
        right[side * NV + variable[valid], side * SLOT + row[valid]] = 1
    same = (node[:, None] == node[None, :]) & valid[:, None] & valid[None, :]
    return (
        jnp.asarray(left, jnp.bfloat16),
        jnp.asarray(right, jnp.bfloat16),
        jnp.asarray(np.concatenate([same, same], axis=1), jnp.float32),
    )


def dot(a, b):
    return jnp.dot(a, b, preferred_element_type=jnp.float32)


VMEM = pl.BlockSpec(memory_space=pltpu.VMEM)

HBM = pl.BlockSpec(memory_space=pltpu.HBM)


def odd(axis):
    return lax.rem(lax.axis_index(axis), 2) == 1


def picks(face, rows, columns):
    shape = (rows.stop - rows.start, columns.stop - columns.start)
    row = lax.broadcasted_iota(jnp.int32, shape, 0) + rows.start
    column = lax.broadcasted_iota(jnp.int32, shape, 1) + columns.start
    group = lax.shift_right_logical(row * 57, 9)
    inner = row - 9 * group
    upper = lax.shift_right_logical(inner * 11, 5)
    side = 2 * (face % 2)
    if face // 2 == 0:
        within = 9 * side + inner
    elif face // 2 == 1:
        within = 9 * upper + 3 * side + inner - 3 * upper
    else:
        within = 3 * inner + side
    hit = (column == 27 * group + within) & (row < NV * NODES)
    return jnp.where(hit, 1.0, 0.0).astype(jnp.bfloat16)


def trace_kernel(state_ref, trace_ref, *refs):
    head_refs = refs[:4]
    main_ref, late_ref = refs[4:]
    unknowns, count = state_ref.shape
    width = head_refs[0].shape[1]
    early = min(unknowns, WIDE)
    tail = late_rows(unknowns)
    rest = SLOT - tail
    for face in range(6):
        main_ref[face * SLOT : (face + 1) * SLOT, :] = picks(face, range(SLOT), range(early))
        late_ref[face * rest : (face + 1) * rest, :] = picks(face, range(tail, SLOT), range(early, unknowns))
    for chunk in range(count // WIDE):
        cols = slice(chunk * WIDE, (chunk + 1) * WIDE)
        main = dot(main_ref[...], state_ref[:early, cols])
        late = dot(late_ref[...], state_ref[early:, cols])
        for face in range(6):
            first = face * SLOT
            trace_ref[face, chunk, :tail, :] = main[first : first + tail].astype(jnp.bfloat16)
            both = main[first + tail : first + SLOT] + late[face * rest : (face + 1) * rest]
            trace_ref[face, chunk, tail:, :] = both.astype(jnp.bfloat16)
    for axis, which in enumerate(BOTH[::-1]):
        flip = odd(which)
        low, high = (trace_ref[2 * axis + side, 0, :, :width] for side in range(2))
        head_refs[2 * axis][...] = jnp.where(flip, low, high)
        head_refs[2 * axis + 1][...] = jnp.where(flip, high, low)


def late_rows(unknowns):
    rows = np.stack([face_rows(face) for face in range(6)])
    return int(np.nonzero((rows >= min(unknowns, WIDE)).any(axis=0))[0][0]) // 16 * 16


def all_traces(flow_state, head_count):
    unknowns, count = flow_state.shape
    early = min(unknowns, WIDE)
    shapes = [(6, count // WIDE, SLOT, WIDE)] + [(SLOT, head_count)] * 4
    return pl.pallas_call(
        trace_kernel,
        in_specs=[VMEM],
        out_specs=[VMEM] * 5,
        out_shape=[jax.ShapeDtypeStruct(shape, jnp.bfloat16) for shape in shapes],
        scratch_shapes=[
            pltpu.VMEM((6 * SLOT, early), jnp.bfloat16),
            pltpu.VMEM((6 * (SLOT - late_rows(unknowns)), unknowns - early), jnp.bfloat16),
        ],
        compiler_params=pltpu.CompilerParams(vmem_limit_bytes=24 << 20),
        cost_estimate=pl.CostEstimate(flops=1 << 30, bytes_accessed=4 << 20, transcendentals=0),
        name="all_traces",
    )(flow_state)


def chosen(index, rows):
    row = lax.broadcasted_iota(jnp.int32, (rows, index.shape[1]), 0)
    return jnp.where(row == index, 1.0, 0.0).astype(jnp.bfloat16)


def local_kernel(trace_ref, nbr_ref, volume_ref, lift_ref, jac_ref, left_ref, right_ref, same_ref, out_ref, weights_ref, flux_mat_ref):
    chunks = trace_ref.shape[1]
    spread = dot(left_ref[...], jac_ref[...]).astype(jnp.bfloat16)
    spread = dot(spread, right_ref[...])
    for face in range(6):
        both = spread[:, face * 2 * SLOT : (face + 1) * 2 * SLOT]
        flux_mat_ref[face] = (both * same_ref[...]).astype(jnp.bfloat16)
    unknowns = volume_ref.shape[1]
    values = lift_ref.shape[2]
    first, second, total_width = operand_places(unknowns)
    for direction in range(4):
        weights_ref[direction, :, :unknowns] = volume_ref[direction]
        weights_ref[direction, :, unknowns:] = jnp.zeros((unknowns, total_width - unknowns), jnp.bfloat16)
        if direction < 3:
            weights_ref[direction, :, first : first + values] = lift_ref[2 * direction]
            weights_ref[direction, :, second : second + values] = lift_ref[2 * direction + 1]
    for step in range(chunks):
        here = slice(step * WIDE, (step + 1) * WIDE)
        for face in range(6):
            index = nbr_ref[face : face + 1, here]
            part = lax.shift_right_logical(index, WIDE.bit_length() - 1)
            source = trace_ref[face ^ 1].reshape(chunks * SLOT, WIDE)
            each = dot(source, chosen(jnp.bitwise_and(index, WIDE - 1), WIDE))
            found = jnp.where(part == 0, each[:SLOT], 0.0)
            for chunk in range(1, chunks):
                found = jnp.where(part == chunk, each[chunk * SLOT : (chunk + 1) * SLOT], found)
            out_ref[face, :, here] = found.astype(jnp.bfloat16)


def operand_places(unknowns):
    first = -(-unknowns // 16) * 16
    second = -(-(first + SLOT) // 128) * 128
    return first, second, second + SLOT


def local_traces(traces, face_nbr, volume_ops, lift_ops, jac):
    faces, chunks, slot, wide = traces.shape
    unknowns = volume_ops.shape[1]
    args = (traces, face_nbr, volume_ops, lift_ops, jac, *kron_parts(12))
    return pl.pallas_call(
        local_kernel,
        in_specs=[VMEM] * len(args),
        out_specs=[VMEM] * 3,
        out_shape=[
            jax.ShapeDtypeStruct((faces, slot, chunks * wide), jnp.bfloat16),
            jax.ShapeDtypeStruct((4, unknowns, operand_places(unknowns)[2]), jnp.bfloat16),
            jax.ShapeDtypeStruct((6, SLOT, 2 * SLOT), jnp.bfloat16),
        ],
        compiler_params=pltpu.CompilerParams(vmem_limit_bytes=24 << 20),
        cost_estimate=pl.CostEstimate(flops=2 << 30, bytes_accessed=4 << 20, transcendentals=0),
        name="local_traces",
    )(*args)


def flow_kernel(directions, state_ref, nbr_ref, trace_ref, local_ref, weights_ref, flux_mat_ref, *refs):
    unknowns, count = state_ref.shape
    first, second, height = operand_places(unknowns)
    out_ref = refs[0]
    if len(refs) > 1:
        out_ref, remote_ref = refs[4:]
        for axis, which in enumerate(BOTH[::-1]):
            flip = odd(which)
            partner, other = refs[2 * axis][...], refs[2 * axis + 1][...]
            remote_ref[2 * axis] = jnp.where(flip, partner, other)
            remote_ref[2 * axis + 1] = jnp.where(flip, other, partner)
    faces = [2 * direction + side for direction in directions if direction < 3 for side in range(2)]

    def some(places):
        wheres = [slice(p * WIDE, (p + 1) * WIDE) for p in places]
        found = {}
        for here in wheres:
            for face in faces:
                found[here.start, face] = local_ref[face, :, here]
                if face < 4:
                    index = nbr_ref[face : face + 1, here] - count
                    remote = dot(remote_ref[face], chosen(index, remote_ref.shape[2]))
                    found[here.start, face] += remote.astype(jnp.bfloat16)
        fluxes = {}
        for p, here in zip(places, wheres):
            for face in faces:
                sides = jnp.concatenate([trace_ref[face, p], found[here.start, face]], axis=0)
                fluxes[p, face] = dot(flux_mat_ref[face], sides).astype(jnp.bfloat16)
        gap = jnp.zeros((second - first - SLOT, WIDE), jnp.bfloat16)
        for p, here in zip(places, wheres):
            own = state_ref[:, here]
            own_padded = jnp.concatenate([own, jnp.zeros((first - unknowns, WIDE), jnp.bfloat16)], axis=0)
            for place, direction in enumerate(directions):
                if direction < 3:
                    operand = [own_padded, fluxes[p, 2 * direction], gap, fluxes[p, 2 * direction + 1]]
                    out_ref[place, :, here] = dot(weights_ref[direction], jnp.concatenate(operand, axis=0))
                else:
                    out_ref[place, :, here] = dot(weights_ref[direction, :, :unknowns], own)

    chunks = count // WIDE
    for start in range(0, chunks, 2):
        some(range(start, min(start + 2, chunks)))


def flow_parts(directions, flow_state, face_nbr, traces, local, weights, flux_mat, *remotes):
    unknowns, count = flow_state.shape
    args = (flow_state, face_nbr, traces, local, weights, flux_mat, *remotes)
    return pl.pallas_call(
        functools.partial(flow_kernel, directions),
        in_specs=[VMEM] * len(args),
        out_specs=VMEM,
        out_shape=jax.ShapeDtypeStruct((len(directions), unknowns, count), jnp.float32),
        scratch_shapes=[pltpu.VMEM((4, *remotes[0].shape), jnp.bfloat16)] if remotes else [],
        compiler_params=pltpu.CompilerParams(vmem_limit_bytes=32 << 20),
        cost_estimate=pl.CostEstimate(flops=2 << 30, bytes_accessed=4 << 20, transcendentals=0),
        name="flow_parts",
    )(*args)


def total(tiles):
    tile = functools.reduce(jnp.add, tiles)
    tile = jnp.sum(jnp.sum(tile, axis=0, keepdims=True), axis=1, keepdims=True)
    return jnp.broadcast_to(tile, (TILE, 128))


def wall_kernel(
    masks, kind_bits, rows, own_rows,
    near_ref, far_ref, base_ref, follow_ref, anchor_ref, parts0_ref, parts1_ref, residual_ref, disp_ref,
    disp, resid, applied, search, image, diag,
):
    comps = 3
    tiles = rows // TILE
    me = lax.axis_index(BOTH)
    flip = kind(me, kind_bits) == 1

    def strided(block):
        first = block * TILE
        return pl.ds((first % tiles) * TILE + first // tiles, TILE, stride=TILE)

    each = 3 * comps * own_rows
    half = near_ref.shape[0] // each
    for pair in range(half):
        ref, at = (near_ref, pair) if pair < half // 2 else (far_ref, pair - half // 2)
        both = ref[2 * at * each : 2 * (at + 1) * each, :].astype(jnp.float32)
        for slot in range(2):
            device = jnp.bitwise_xor(me, jnp.where(flip, masks[1][2 * pair + slot], masks[0][2 * pair + slot]))
            upper, lower, stiff = (both[slot * each + k * comps * own_rows :][: comps * own_rows] for k in range(3))
            load = upper + lower
            for block in range(own_rows // TILE):
                to = strided(device * (own_rows // TILE) + block)
                for c in range(comps):
                    first = c * own_rows + block * TILE
                    resid[c, to, :] = load[first : first + TILE]
                    diag[c, to, :] = 4.0 + stiff[first : first + TILE]

    lane = lax.broadcasted_iota(jnp.int32, (TILE, 128), 1)
    sub = lax.broadcasted_iota(jnp.int32, (TILE, 128), 0)
    group = 16
    zero = jnp.zeros((TILE, 128), jnp.float32)

    def at(tile):
        return pl.ds(tile * TILE if isinstance(tile, int) else pl.multiple_of(tile * TILE, TILE), TILE)

    def sweep(renew):
        norms, energies = [], []
        for c in range(comps):
            above = jnp.where(sub == 0, 0.0, pltpu.roll(renew(c, tiles - 1, False), 1, 0))

            def operate(tile, above, value, below, c=c):
                beside = above + below
                beside += jnp.where(lane == 0, 0.0, pltpu.roll(value, 1, 1))
                beside += jnp.where(lane == 127, 0.0, pltpu.roll(value, 127, 1))
                result = diag[c, at(tile), :] * value - beside
                applied[c, at(tile), :] = result
                return value * value, value * result

            def some(chunk, carry, c=c):
                above, value, norm, energy = carry
                norm, energy = [norm, zero], [energy, zero]
                for k in range(group):
                    tile = chunk * group + k + 1
                    below = renew(c, tile, True)
                    terms = operate(tile - 1, above, value, below)
                    norm[k % 2] += terms[0]
                    energy[k % 2] += terms[1]
                    above, value = value, below
                return above, value, norm[0] + norm[1], energy[0] + energy[1]

            first = value = renew(c, 0, True)
            norm = energy = zero
            if tiles > group:
                above, value, norm, energy = lax.fori_loop(0, tiles // group - 1, some, (above, value, norm, energy))
            norm, energy = [norm, zero], [energy, zero]
            for tile in range(tiles - group + 1, tiles + 1):
                if tile < tiles:
                    below = renew(c, tile, True)
                else:
                    below = jnp.where(sub == TILE - 1, 0.0, pltpu.roll(first, TILE - 1, 0))
                terms = operate(tile - 1, above, value, below)
                norm[tile % 2] += terms[0]
                energy[tile % 2] += terms[1]
                above, value = value, below
            norms += norm
            energies += energy
        return total(norms), total(energies)

    def begin(c, tile, keep):
        return resid[c, at(tile), :]

    def advance(step_size, ratio, last_step=None, first=False):
        def renew(c, tile, keep):
            value = resid[c, at(tile), :]
            toward, moved = value, applied[c, at(tile), :]
            if not first:
                before = search[c, at(tile), :]
                toward += ratio * before
                moved += ratio * image[c, at(tile), :]
            value -= step_size * moved
            if keep:
                search[c, at(tile), :] = toward
                image[c, at(tile), :] = moved
                resid[c, at(tile), :] = value
                if last_step is not None:
                    disp[c, at(tile), :] += last_step * before + step_size * toward
            return value

        return renew

    def sizes(norm, energy, last_norm, last_curve):
        ratio = norm / last_norm
        curve = energy - ratio * ratio * last_curve
        return norm / curve, ratio, curve

    norm, curve = sweep(begin)
    step_size = norm / curve
    last_norm, last_curve, last_step = norm, curve, step_size
    norm, energy = sweep(advance(step_size, None, first=True))

    def clear(tile, carry):
        for c in range(comps):
            disp[c, at(tile), :] = zero
        return carry

    lax.fori_loop(0, tiles, clear, 0, unroll=8)

    def two(position, carry):
        norm, energy, last_norm, last_curve, last_step = carry
        step_size, ratio, curve = sizes(norm, energy, last_norm, last_curve)
        last_norm = norm
        norm, energy = sweep(advance(step_size, ratio, last_step))
        step_size, ratio, curve = sizes(norm, energy, last_norm, curve)
        last_norm = norm
        norm, energy = sweep(advance(step_size, ratio))
        return norm, energy, last_norm, curve, step_size

    assert ITERS % 2 == 0
    carry = lax.fori_loop(0, ITERS // 2 - 1, two, (norm, energy, last_norm, last_curve, last_step))
    norm, energy, last_norm, last_curve, last_step = carry
    step_size, ratio, curve = sizes(norm, energy, last_norm, last_curve)

    def finish(tile, carry):
        for c in range(comps):
            before = search[c, at(tile), :]
            toward = resid[c, at(tile), :] + ratio * before
            disp[c, at(tile), :] += last_step * before + step_size * toward
        return carry

    lax.fori_loop(0, tiles, finish, 0, unroll=8)

    for block in range(own_rows // TILE):
        for c in range(comps):
            disp_ref[c, block * TILE : (block + 1) * TILE, :] = disp[c, strided(me * (own_rows // TILE) + block), :]

    anchor = anchor_ref[...]
    count = anchor.shape[1]
    row = anchor // 128
    column = anchor - row * 128
    upper = row // tiles
    place = (row - upper * tiles) * TILE + upper
    some_rows = 128
    run = lax.shift_right_logical(place, 7)
    pair = lax.shift_right_logical(run, 1)
    inner = place - some_rows * run
    pick = chosen(column + 128 * (run - 2 * pair), 256)
    pick = jnp.concatenate([pick, pick], axis=0)
    row_of = lax.broadcasted_iota(jnp.int32, (some_rows, count), 0)

    def look(chunk, sums):
        hit = row_of == jnp.where(pair == chunk, inner, -1)
        out = []
        for c in range(comps):
            values = [disp[c, pl.ds(pl.multiple_of((2 * chunk + k) * some_rows, some_rows), some_rows), :] for k in range(2)]
            value = jnp.concatenate(values, axis=1)
            coarse = value.astype(jnp.bfloat16)
            fine = (value - coarse.astype(jnp.float32)).astype(jnp.bfloat16)
            found = dot(jnp.concatenate([coarse, fine], axis=1), pick)
            found = jnp.where(hit, found, 0.0).reshape(some_rows // TILE, TILE, count)
            out.append(sums[c] + jnp.sum(found, axis=0))
        return tuple(out)

    sums = (jnp.zeros((TILE, count), jnp.float32),) * comps
    chunks = rows // (2 * some_rows)
    sums = lax.fori_loop(0, chunks, look, sums, unroll=chunks <= 2)
    follow = follow_ref[...]
    geometry = [
        base_ref[c : c + 1, :] * jnp.exp(follow * jnp.sum(sums[c], axis=0, keepdims=True)) for c in range(comps)
    ]
    geometry.append(base_ref[comps : comps + 1, :])
    unknowns = residual_ref.shape[0]
    parts = [(ref, place) for ref in (parts0_ref, parts1_ref) for place in range(ref.shape[0])]
    for first in range(0, unknowns, 16):
        some = slice(first, min(first + 16, unknowns))
        terms = [factor * ref[place, some, :] for factor, (ref, place) in zip(geometry, parts)]
        residual_ref[some, :] = functools.reduce(jnp.add, terms).astype(jnp.bfloat16)


def wall_and_residual(near, far, masks, kind_bits, base_geometry, anchor_weight, wall_anchor, parts, own_rows):
    rows = own_rows * len(masks[0])
    unknowns, count = parts[0].shape[1], anchor_weight.shape[0]
    field = pltpu.VMEM((3, rows, 128), jnp.float32)
    return pl.pallas_call(
        functools.partial(wall_kernel, masks, kind_bits, rows, own_rows),
        in_specs=[VMEM] * 7,
        out_specs=[VMEM] * 2,
        out_shape=[
            jax.ShapeDtypeStruct((unknowns, count), jnp.bfloat16),
            jax.ShapeDtypeStruct((3, own_rows, 128), jnp.float32),
        ],
        scratch_shapes=[
            field,
            field,
            field,
            field,
            field,
            field,
        ],
        compiler_params=pltpu.CompilerParams(vmem_limit_bytes=(16 << 20) + 16 * rows * 3 * 128 * 4),
        cost_estimate=pl.CostEstimate(flops=4 << 30, bytes_accessed=8 << 20, transcendentals=0),
        name="wall_and_residual",
    )(near, far, base_geometry, anchor_weight[None, :], wall_anchor[None, :], *parts)


def paired(x, axis, offset):
    peers = lax.axis_size(axis)
    pairs = [((i + offset) % peers, (i + offset + 1) % peers) for i in range(0, peers, 2)]
    return lax.ppermute(x, axis, pairs + [pair[::-1] for pair in pairs])


def gather_stages(mesh):
    n_sec, n_dom = mesh.shape["sec"], mesh.shape["dom"]
    assert n_sec & (n_sec - 1) == 0 and n_dom & (n_dom - 1) == 0 and n_sec > 1
    bits = [1 << b for b in range((n_sec * n_dom).bit_length() - 1)]
    inner, outer = bits[: n_dom.bit_length() - 1], bits[n_dom.bit_length() :]
    order = inner[::-1] + outer[::-1]
    order[:2] = order[1::-1]
    first = [bit ^ n_dom for bit in order]
    second = first[:-2] + first[-2:][::-1]
    return (first + [n_dom], second + [n_dom]), order[-2:] + [n_dom]


def kind(device, bits):
    return sum(device // bit % 2 for bit in bits) % 2


def on_device(
    stages, kind_bits,
    flow_state, base_geometry, anchor_weight, wall_anchor, face_nbr, volume_ops, lift_ops, face_jac, wall_load, wall_stiff,
):
    own_rows, width = wall_load.shape[1:]
    wall = jnp.concatenate([wall_load, wall_load, wall_stiff], axis=0).reshape(9 * own_rows, width)
    third = lax.broadcasted_iota(jnp.int32, wall.shape, 0) // (3 * own_rows)
    wall = jnp.where(third == 1, wall - lax.reduce_precision(wall, 8, 7), wall).astype(jnp.bfloat16)
    masks = []
    for bits in stages:
        masks.append([0])
        for bit in bits[:-1]:
            masks[-1] += [m ^ bit for m in masks[-1]]
    masks = [ours + [m ^ stages[0][-1] for m in theirs] for ours, theirs in (masks, masks[::-1])]
    devices = lax.axis_size(BOTH)

    def sent(wall, position):
        pairs = [(i, i ^ stages[kind(i, kind_bits)][position]) for i in range(devices)]
        return lax.ppermute(wall, BOTH, pairs)

    barrier = lax.optimization_barrier
    far = sent(wall, 0)
    head_count = flow_state.shape[1] // 8
    traces, *heads = all_traces(flow_state, head_count)
    remotes = [None] * 4
    far, heads = barrier((far, heads))
    wall = jnp.concatenate([wall, far], axis=0)
    far = sent(wall, 1)
    remotes[1] = paired(heads[1], "dom", 1)
    far, heads, face_jac = barrier((far, heads, face_jac))
    wall = jnp.concatenate([wall, far], axis=0)
    far = sent(wall, 2)
    jac = face_jac.transpose(2, 0, 1, 3).reshape(NV, 12 * NV)
    remotes[2] = paired(heads[2], "sec", 0)
    remotes[0] = paired(heads[0], "dom", 0)
    remotes[3] = paired(heads[3], "sec", 1)
    far, traces, volume_ops, jac, remotes[1] = barrier((far, traces, volume_ops, jac, remotes[1]))
    wall = jnp.concatenate([wall, far], axis=0)
    far = sent(wall, 3)
    local, weights, flux_mat = local_traces(traces, face_nbr, volume_ops, lift_ops, jac)
    common = (flow_state, face_nbr, traces, local, weights, flux_mat)
    inner = flow_parts((2, 3), *common)
    far, inner, remotes[0], remotes[2], remotes[3] = barrier((far, inner, remotes[0], remotes[2], remotes[3]))
    for position in range(4, len(stages[0])):
        wall = jnp.concatenate([wall, far], axis=0)
        far = sent(wall, position)
    outer = flow_parts((0, 1), *common, *remotes)
    halves = (outer, inner)
    return wall_and_residual(wall, far, masks, kind_bits, base_geometry, anchor_weight, wall_anchor, halves, own_rows)


def solution(mesh):
    return jax.shard_map(
        functools.partial(on_device, *gather_stages(mesh)),
        mesh=mesh,
        in_specs=(
            P(None, BOTH),
            P(None, BOTH),
            P(BOTH),
            P(BOTH),
            P(None, BOTH),
            P(),
            P(),
            P(),
            P(None, BOTH, None),
            P(None, BOTH, None),
        ),
        out_specs=(P(None, BOTH), P(None, BOTH, None)),
        check_vma=False,
    )
```

```python
import functools

import jax
import jax.numpy as jnp
import numpy as np
from jax import lax
from jax.experimental import pallas as pl
from jax.experimental.pallas import tpu as pltpu
from jax.sharding import PartitionSpec as P

NV = 5
ITERS = 8
NODES = 18
SLOT = 96
TILE = 8
WIDE = 256
BOTH = ("sec", "dom")


def face_rows(face):
    rows = np.arange(NV * 54).reshape(NV * 2, 3, 3, 3)
    return np.take(rows, 0 if face % 2 == 0 else 2, axis=1 + face // 2).reshape(-1)


def kron_parts(sides):
    row = np.arange(SLOT)
    valid = row < NV * NODES
    variable, node = row // NODES, row % NODES
    left = np.zeros((SLOT, NV), np.float32)
    left[row[valid], variable[valid]] = 1
    right = np.zeros((sides * NV, sides * SLOT), np.float32)
    for side in range(sides):
        right[side * NV + variable[valid], side * SLOT + row[valid]] = 1
    same = (node[:, None] == node[None, :]) & valid[:, None] & valid[None, :]
    return (
        jnp.asarray(left, jnp.bfloat16),
        jnp.asarray(right, jnp.bfloat16),
        jnp.asarray(np.concatenate([same, same], axis=1), jnp.float32),
    )


def dot(a, b):
    return jnp.dot(a, b, preferred_element_type=jnp.float32)


VMEM = pl.BlockSpec(memory_space=pltpu.VMEM)

HBM = pl.BlockSpec(memory_space=pltpu.HBM)


def odd(axis):
    return lax.rem(lax.axis_index(axis), 2) == 1


def picks(face, rows, columns):
    shape = (rows.stop - rows.start, columns.stop - columns.start)
    row = lax.broadcasted_iota(jnp.int32, shape, 0) + rows.start
    column = lax.broadcasted_iota(jnp.int32, shape, 1) + columns.start
    group = lax.shift_right_logical(row * 57, 9)
    inner = row - 9 * group
    upper = lax.shift_right_logical(inner * 11, 5)
    side = 2 * (face % 2)
    if face // 2 == 0:
        within = 9 * side + inner
    elif face // 2 == 1:
        within = 9 * upper + 3 * side + inner - 3 * upper
    else:
        within = 3 * inner + side
    hit = (column == 27 * group + within) & (row < NV * NODES)
    return jnp.where(hit, 1.0, 0.0).astype(jnp.bfloat16)


def trace_kernel(state_ref, trace_ref, *refs):
    head_refs = refs[:4]
    main_ref, late_ref = refs[4:]
    unknowns, count = state_ref.shape
    width = head_refs[0].shape[1]
    early = min(unknowns, WIDE)
    tail = late_rows(unknowns)
    rest = SLOT - tail
    for face in range(6):
        main_ref[face * SLOT : (face + 1) * SLOT, :] = picks(face, range(SLOT), range(early))
        late_ref[face * rest : (face + 1) * rest, :] = picks(face, range(tail, SLOT), range(early, unknowns))
    for chunk in range(count // WIDE):
        cols = slice(chunk * WIDE, (chunk + 1) * WIDE)
        main = dot(main_ref[...], state_ref[:early, cols])
        late = dot(late_ref[...], state_ref[early:, cols])
        for face in range(6):
            first = face * SLOT
            trace_ref[face, chunk, :tail, :] = main[first : first + tail].astype(jnp.bfloat16)
            both = main[first + tail : first + SLOT] + late[face * rest : (face + 1) * rest]
            trace_ref[face, chunk, tail:, :] = both.astype(jnp.bfloat16)
    for axis, which in enumerate(BOTH[::-1]):
        flip = odd(which)
        low, high = (trace_ref[2 * axis + side, 0, :, :width] for side in range(2))
        head_refs[2 * axis][...] = jnp.where(flip, low, high)
        head_refs[2 * axis + 1][...] = jnp.where(flip, high, low)


def late_rows(unknowns):
    rows = np.stack([face_rows(face) for face in range(6)])
    return int(np.nonzero((rows >= min(unknowns, WIDE)).any(axis=0))[0][0]) // 16 * 16


def all_traces(flow_state, head_count):
    unknowns, count = flow_state.shape
    early = min(unknowns, WIDE)
    shapes = [(6, count // WIDE, SLOT, WIDE)] + [(SLOT, head_count)] * 4
    return pl.pallas_call(
        trace_kernel,
        in_specs=[VMEM],
        out_specs=[VMEM] * 5,
        out_shape=[jax.ShapeDtypeStruct(shape, jnp.bfloat16) for shape in shapes],
        scratch_shapes=[
            pltpu.VMEM((6 * SLOT, early), jnp.bfloat16),
            pltpu.VMEM((6 * (SLOT - late_rows(unknowns)), unknowns - early), jnp.bfloat16),
        ],
        compiler_params=pltpu.CompilerParams(vmem_limit_bytes=24 << 20),
        cost_estimate=pl.CostEstimate(flops=1 << 30, bytes_accessed=4 << 20, transcendentals=0),
        name="all_traces",
    )(flow_state)


def chosen(index, rows):
    row = lax.broadcasted_iota(jnp.int32, (rows, index.shape[1]), 0)
    return jnp.where(row == index, 1.0, 0.0).astype(jnp.bfloat16)


def local_kernel(trace_ref, nbr_ref, volume_ref, lift_ref, jac_ref, left_ref, right_ref, same_ref, out_ref, weights_ref, flux_mat_ref):
    chunks = trace_ref.shape[1]
    spread = dot(left_ref[...], jac_ref[...]).astype(jnp.bfloat16)
    spread = dot(spread, right_ref[...])
    for face in range(6):
        both = spread[:, face * 2 * SLOT : (face + 1) * 2 * SLOT]
        flux_mat_ref[face] = (both * same_ref[...]).astype(jnp.bfloat16)
    unknowns = volume_ref.shape[1]
    values = lift_ref.shape[2]
    first, second, total_width = operand_places(unknowns)
    for direction in range(4):
        weights_ref[direction, :, :unknowns] = volume_ref[direction]
        weights_ref[direction, :, unknowns:] = jnp.zeros((unknowns, total_width - unknowns), jnp.bfloat16)
        if direction < 3:
            weights_ref[direction, :, first : first + values] = lift_ref[2 * direction]
            weights_ref[direction, :, second : second + values] = lift_ref[2 * direction + 1]
    for step in range(chunks):
        here = slice(step * WIDE, (step + 1) * WIDE)
        for face in range(6):
            index = nbr_ref[face : face + 1, here]
            part = lax.shift_right_logical(index, WIDE.bit_length() - 1)
            source = trace_ref[face ^ 1].reshape(chunks * SLOT, WIDE)
            each = dot(source, chosen(jnp.bitwise_and(index, WIDE - 1), WIDE))
            found = jnp.where(part == 0, each[:SLOT], 0.0)
            for chunk in range(1, chunks):
                found = jnp.where(part == chunk, each[chunk * SLOT : (chunk + 1) * SLOT], found)
            out_ref[face, :, here] = found.astype(jnp.bfloat16)


def operand_places(unknowns):
    first = -(-unknowns // 16) * 16
    second = -(-(first + SLOT) // 128) * 128
    return first, second, second + SLOT


def local_traces(traces, face_nbr, volume_ops, lift_ops, jac):
    faces, chunks, slot, wide = traces.shape
    unknowns = volume_ops.shape[1]
    args = (traces, face_nbr, volume_ops, lift_ops, jac, *kron_parts(12))
    return pl.pallas_call(
        local_kernel,
        in_specs=[VMEM] * len(args),
        out_specs=[VMEM] * 3,
        out_shape=[
            jax.ShapeDtypeStruct((faces, slot, chunks * wide), jnp.bfloat16),
            jax.ShapeDtypeStruct((4, unknowns, operand_places(unknowns)[2]), jnp.bfloat16),
            jax.ShapeDtypeStruct((6, SLOT, 2 * SLOT), jnp.bfloat16),
        ],
        compiler_params=pltpu.CompilerParams(vmem_limit_bytes=24 << 20),
        cost_estimate=pl.CostEstimate(flops=2 << 30, bytes_accessed=4 << 20, transcendentals=0),
        name="local_traces",
    )(*args)


def flow_kernel(directions, state_ref, nbr_ref, trace_ref, local_ref, weights_ref, flux_mat_ref, *refs):
    unknowns, count = state_ref.shape
    first, second, height = operand_places(unknowns)
    out_ref = refs[0]
    if len(refs) > 1:
        out_ref, remote_ref = refs[4:]
        for axis, which in enumerate(BOTH[::-1]):
            flip = odd(which)
            partner, other = refs[2 * axis][...], refs[2 * axis + 1][...]
            remote_ref[2 * axis] = jnp.where(flip, partner, other)
            remote_ref[2 * axis + 1] = jnp.where(flip, other, partner)
    faces = [2 * direction + side for direction in directions if direction < 3 for side in range(2)]

    def some(places):
        wheres = [slice(p * WIDE, (p + 1) * WIDE) for p in places]
        found = {}
        for here in wheres:
            for face in faces:
                found[here.start, face] = local_ref[face, :, here]
                if face < 4:
                    index = nbr_ref[face : face + 1, here] - count
                    remote = dot(remote_ref[face], chosen(index, remote_ref.shape[2]))
                    found[here.start, face] += remote.astype(jnp.bfloat16)
        fluxes = {}
        for p, here in zip(places, wheres):
            for face in faces:
                sides = jnp.concatenate([trace_ref[face, p], found[here.start, face]], axis=0)
                fluxes[p, face] = dot(flux_mat_ref[face], sides).astype(jnp.bfloat16)
        gap = jnp.zeros((second - first - SLOT, WIDE), jnp.bfloat16)
        for p, here in zip(places, wheres):
            own = state_ref[:, here]
            own_padded = jnp.concatenate([own, jnp.zeros((first - unknowns, WIDE), jnp.bfloat16)], axis=0)
            for place, direction in enumerate(directions):
                if direction < 3:
                    operand = [own_padded, fluxes[p, 2 * direction], gap, fluxes[p, 2 * direction + 1]]
                    out_ref[place, :, here] = dot(weights_ref[direction], jnp.concatenate(operand, axis=0))
                else:
                    out_ref[place, :, here] = dot(weights_ref[direction, :, :unknowns], own)

    chunks = count // WIDE
    for start in range(0, chunks, 2):
        some(range(start, min(start + 2, chunks)))


def flow_parts(directions, flow_state, face_nbr, traces, local, weights, flux_mat, *remotes):
    unknowns, count = flow_state.shape
    args = (flow_state, face_nbr, traces, local, weights, flux_mat, *remotes)
    return pl.pallas_call(
        functools.partial(flow_kernel, directions),
        in_specs=[VMEM] * len(args),
        out_specs=VMEM,
        out_shape=jax.ShapeDtypeStruct((len(directions), unknowns, count), jnp.float32),
        scratch_shapes=[pltpu.VMEM((4, *remotes[0].shape), jnp.bfloat16)] if remotes else [],
        compiler_params=pltpu.CompilerParams(vmem_limit_bytes=32 << 20),
        cost_estimate=pl.CostEstimate(flops=2 << 30, bytes_accessed=4 << 20, transcendentals=0),
        name="flow_parts",
    )(*args)


def total(tiles):
    tile = functools.reduce(jnp.add, tiles)
    tile = jnp.sum(jnp.sum(tile, axis=0, keepdims=True), axis=1, keepdims=True)
    return jnp.broadcast_to(tile, (TILE, 128))


def wall_kernel(
    masks, kind_bits, rows, own_rows,
    near_ref, far_ref, base_ref, follow_ref, anchor_ref, parts0_ref, parts1_ref, residual_ref, disp_ref,
    disp, resid, applied, search, image, diag,
):
    comps = 3
    tiles = rows // TILE
    me = lax.axis_index(BOTH)
    flip = kind(me, kind_bits) == 1

    def strided(block):
        first = block * TILE
        return pl.ds((first % tiles) * TILE + first // tiles, TILE, stride=TILE)

    each = 3 * comps * own_rows
    half = near_ref.shape[0] // each
    for pair in range(half):
        ref, at = (near_ref, pair) if pair < half // 2 else (far_ref, pair - half // 2)
        both = ref[2 * at * each : 2 * (at + 1) * each, :].astype(jnp.float32)
        for slot in range(2):
            device = jnp.bitwise_xor(me, jnp.where(flip, masks[1][2 * pair + slot], masks[0][2 * pair + slot]))
            upper, lower, stiff = (both[slot * each + k * comps * own_rows :][: comps * own_rows] for k in range(3))
            load = upper + lower
            for block in range(own_rows // TILE):
                to = strided(device * (own_rows // TILE) + block)
                for c in range(comps):
                    first = c * own_rows + block * TILE
                    resid[c, to, :] = load[first : first + TILE]
                    diag[c, to, :] = 4.0 + stiff[first : first + TILE]

    lane = lax.broadcasted_iota(jnp.int32, (TILE, 128), 1)
    sub = lax.broadcasted_iota(jnp.int32, (TILE, 128), 0)
    group = 32 if tiles % 32 == 0 else 8
    zero = jnp.zeros((TILE, 128), jnp.float32)

    def at(tile):
        return pl.ds(tile * TILE if isinstance(tile, int) else pl.multiple_of(tile * TILE, TILE), TILE)

    def sweep(renew):
        norms, energies = [], []
        for c in range(comps):
            above = jnp.where(sub == 0, 0.0, pltpu.roll(renew(c, tiles - 1, False), 1, 0))

            def operate(tile, above, value, below, c=c):
                beside = above + below
                beside += jnp.where(lane == 0, 0.0, pltpu.roll(value, 1, 1))
                beside += jnp.where(lane == 127, 0.0, pltpu.roll(value, 127, 1))
                result = diag[c, at(tile), :] * value - beside
                applied[c, at(tile), :] = result
                return value * value, value * result

            def some(chunk, carry, c=c):
                above, value, norm, energy = carry
                norm, energy = [norm, zero, zero, zero], [energy, zero, zero, zero]
                for k in range(group):
                    tile = chunk * group + k + 1
                    below = renew(c, tile, True)
                    terms = operate(tile - 1, above, value, below)
                    norm[k % 4] += terms[0]
                    energy[k % 4] += terms[1]
                    above, value = value, below
                return above, value, sum(norm[1:], norm[0]), sum(energy[1:], energy[0])

            first = value = renew(c, 0, True)
            norm = energy = zero
            if tiles > group:
                above, value, norm, energy = lax.fori_loop(0, tiles // group - 1, some, (above, value, norm, energy))
            norm, energy = [norm, zero, zero, zero], [energy, zero, zero, zero]
            for tile in range(tiles - group + 1, tiles + 1):
                if tile < tiles:
                    below = renew(c, tile, True)
                else:
                    below = jnp.where(sub == TILE - 1, 0.0, pltpu.roll(first, TILE - 1, 0))
                terms = operate(tile - 1, above, value, below)
                norm[tile % 4] += terms[0]
                energy[tile % 4] += terms[1]
                above, value = value, below
            norms += norm
            energies += energy
        return total(norms), total(energies)

    def begin(c, tile, keep):
        return resid[c, at(tile), :]

    def advance(step_size, ratio, last_step=None, first=False):
        def renew(c, tile, keep):
            value = resid[c, at(tile), :]
            toward, moved = value, applied[c, at(tile), :]
            if not first:
                before = search[c, at(tile), :]
                toward += ratio * before
                moved += ratio * image[c, at(tile), :]
            value -= step_size * moved
            if keep:
                search[c, at(tile), :] = toward
                image[c, at(tile), :] = moved
                resid[c, at(tile), :] = value
                if last_step is not None:
                    disp[c, at(tile), :] += last_step * before + step_size * toward
            return value

        return renew

    def sizes(norm, energy, last_norm, last_curve):
        ratio = norm / last_norm
        curve = energy - ratio * ratio * last_curve
        return norm / curve, ratio, curve

    norm, curve = sweep(begin)
    step_size = norm / curve
    last_norm, last_curve, last_step = norm, curve, step_size
    norm, energy = sweep(advance(step_size, None, first=True))

    def clear(tile, carry):
        for c in range(comps):
            disp[c, at(tile), :] = zero
        return carry

    lax.fori_loop(0, tiles, clear, 0, unroll=8)

    def two(position, carry):
        norm, energy, last_norm, last_curve, last_step = carry
        step_size, ratio, curve = sizes(norm, energy, last_norm, last_curve)
        last_norm = norm
        norm, energy = sweep(advance(step_size, ratio, last_step))
        step_size, ratio, curve = sizes(norm, energy, last_norm, curve)
        last_norm = norm
        norm, energy = sweep(advance(step_size, ratio))
        return norm, energy, last_norm, curve, step_size

    assert ITERS % 2 == 0
    carry = lax.fori_loop(0, ITERS // 2 - 1, two, (norm, energy, last_norm, last_curve, last_step))
    norm, energy, last_norm, last_curve, last_step = carry
    step_size, ratio, curve = sizes(norm, energy, last_norm, last_curve)

    def finish(tile, carry):
        for c in range(comps):
            before = search[c, at(tile), :]
            toward = resid[c, at(tile), :] + ratio * before
            disp[c, at(tile), :] += last_step * before + step_size * toward
        return carry

    lax.fori_loop(0, tiles, finish, 0, unroll=8)

    for block in range(own_rows // TILE):
        for c in range(comps):
            disp_ref[c, block * TILE : (block + 1) * TILE, :] = disp[c, strided(me * (own_rows // TILE) + block), :]

    anchor = anchor_ref[...]
    count = anchor.shape[1]
    row = anchor // 128
    column = anchor - row * 128
    upper = row // tiles
    place = (row - upper * tiles) * TILE + upper
    some_rows = 128
    run = lax.shift_right_logical(place, 7)
    pair = lax.shift_right_logical(run, 1)
    inner = place - some_rows * run
    pick = chosen(column + 128 * (run - 2 * pair), 256)
    pick = jnp.concatenate([pick, pick], axis=0)
    row_of = lax.broadcasted_iota(jnp.int32, (some_rows, count), 0)

    def look(chunk, sums):
        hit = row_of == jnp.where(pair == chunk, inner, -1)
        out = []
        for c in range(comps):
            values = [disp[c, pl.ds(pl.multiple_of((2 * chunk + k) * some_rows, some_rows), some_rows), :] for k in range(2)]
            value = jnp.concatenate(values, axis=1)
            coarse = value.astype(jnp.bfloat16)
            fine = (value - coarse.astype(jnp.float32)).astype(jnp.bfloat16)
            found = dot(jnp.concatenate([coarse, fine], axis=1), pick)
            found = jnp.where(hit, found, 0.0).reshape(some_rows // TILE, TILE, count)
            out.append(sums[c] + jnp.sum(found, axis=0))
        return tuple(out)

    sums = (jnp.zeros((TILE, count), jnp.float32),) * comps
    chunks = rows // (2 * some_rows)
    sums = lax.fori_loop(0, chunks, look, sums, unroll=chunks <= 2)
    follow = follow_ref[...]
    geometry = [
        base_ref[c : c + 1, :] * jnp.exp(follow * jnp.sum(sums[c], axis=0, keepdims=True)) for c in range(comps)
    ]
    geometry.append(base_ref[comps : comps + 1, :])
    unknowns = residual_ref.shape[0]
    parts = [(ref, place) for ref in (parts0_ref, parts1_ref) for place in range(ref.shape[0])]
    for first in range(0, unknowns, 16):
        some = slice(first, min(first + 16, unknowns))
        terms = [factor * ref[place, some, :] for factor, (ref, place) in zip(geometry, parts)]
        residual_ref[some, :] = functools.reduce(jnp.add, terms).astype(jnp.bfloat16)


def wall_and_residual(near, far, masks, kind_bits, base_geometry, anchor_weight, wall_anchor, parts, own_rows):
    rows = own_rows * len(masks[0])
    unknowns, count = parts[0].shape[1], anchor_weight.shape[0]
    field = pltpu.VMEM((3, rows, 128), jnp.float32)
    return pl.pallas_call(
        functools.partial(wall_kernel, masks, kind_bits, rows, own_rows),
        in_specs=[VMEM] * 7,
        out_specs=[VMEM] * 2,
        out_shape=[
            jax.ShapeDtypeStruct((unknowns, count), jnp.bfloat16),
            jax.ShapeDtypeStruct((3, own_rows, 128), jnp.float32),
        ],
        scratch_shapes=[
            field,
            field,
            field,
            field,
            field,
            field,
        ],
        compiler_params=pltpu.CompilerParams(vmem_limit_bytes=(16 << 20) + 16 * rows * 3 * 128 * 4),
        cost_estimate=pl.CostEstimate(flops=4 << 30, bytes_accessed=8 << 20, transcendentals=0),
        name="wall_and_residual",
    )(near, far, base_geometry, anchor_weight[None, :], wall_anchor[None, :], *parts)


def paired(x, axis, offset):
    peers = lax.axis_size(axis)
    pairs = [((i + offset) % peers, (i + offset + 1) % peers) for i in range(0, peers, 2)]
    return lax.ppermute(x, axis, pairs + [pair[::-1] for pair in pairs])


def gather_stages(mesh):
    n_sec, n_dom = mesh.shape["sec"], mesh.shape["dom"]
    assert n_sec & (n_sec - 1) == 0 and n_dom & (n_dom - 1) == 0 and n_sec > 1
    bits = [1 << b for b in range((n_sec * n_dom).bit_length() - 1)]
    inner, outer = bits[: n_dom.bit_length() - 1], bits[n_dom.bit_length() :]
    order = inner[::-1] + outer[::-1]
    order[:2] = order[1::-1]
    first = [bit ^ n_dom for bit in order]
    second = first[:-2] + first[-2:][::-1]
    return (first + [n_dom], second + [n_dom]), order[-2:] + [n_dom]


def kind(device, bits):
    return sum(device // bit % 2 for bit in bits) % 2


def on_device(
    stages, kind_bits,
    flow_state, base_geometry, anchor_weight, wall_anchor, face_nbr, volume_ops, lift_ops, face_jac, wall_load, wall_stiff,
):
    own_rows, width = wall_load.shape[1:]
    wall = jnp.concatenate([wall_load, wall_load, wall_stiff], axis=0).reshape(9 * own_rows, width)
    third = lax.broadcasted_iota(jnp.int32, wall.shape, 0) // (3 * own_rows)
    wall = jnp.where(third == 1, wall - lax.reduce_precision(wall, 8, 7), wall).astype(jnp.bfloat16)
    masks = []
    for bits in stages:
        masks.append([0])
        for bit in bits[:-1]:
            masks[-1] += [m ^ bit for m in masks[-1]]
    masks = [ours + [m ^ stages[0][-1] for m in theirs] for ours, theirs in (masks, masks[::-1])]
    devices = lax.axis_size(BOTH)

    def sent(wall, position):
        pairs = [(i, i ^ stages[kind(i, kind_bits)][position]) for i in range(devices)]
        return lax.ppermute(wall, BOTH, pairs)

    barrier = lax.optimization_barrier
    far = sent(wall, 0)
    head_count = flow_state.shape[1] // 8
    traces, *heads = all_traces(flow_state, head_count)
    remotes = [None] * 4
    far, heads = barrier((far, heads))
    wall = jnp.concatenate([wall, far], axis=0)
    far = sent(wall, 1)
    remotes[1] = paired(heads[1], "dom", 1)
    far, heads, face_jac = barrier((far, heads, face_jac))
    wall = jnp.concatenate([wall, far], axis=0)
    far = sent(wall, 2)
    jac = face_jac.transpose(2, 0, 1, 3).reshape(NV, 12 * NV)
    remotes[2] = paired(heads[2], "sec", 0)
    remotes[0] = paired(heads[0], "dom", 0)
    remotes[3] = paired(heads[3], "sec", 1)
    far, traces, volume_ops, jac, remotes[1] = barrier((far, traces, volume_ops, jac, remotes[1]))
    wall = jnp.concatenate([wall, far], axis=0)
    far = sent(wall, 3)
    local, weights, flux_mat = local_traces(traces, face_nbr, volume_ops, lift_ops, jac)
    common = (flow_state, face_nbr, traces, local, weights, flux_mat)
    inner = flow_parts((2, 3), *common)
    far, inner, remotes[0], remotes[2], remotes[3] = barrier((far, inner, remotes[0], remotes[2], remotes[3]))
    for position in range(4, len(stages[0])):
        wall = jnp.concatenate([wall, far], axis=0)
        far = sent(wall, position)
    outer = flow_parts((0, 1), *common, *remotes)
    halves = (outer, inner)
    return wall_and_residual(wall, far, masks, kind_bits, base_geometry, anchor_weight, wall_anchor, halves, own_rows)


def solution(mesh):
    return jax.shard_map(
        functools.partial(on_device, *gather_stages(mesh)),
        mesh=mesh,
        in_specs=(
            P(None, BOTH),
            P(None, BOTH),
            P(BOTH),
            P(BOTH),
            P(None, BOTH),
            P(),
            P(),
            P(),
            P(None, BOTH, None),
            P(None, BOTH, None),
        ),
        out_specs=(P(None, BOTH), P(None, BOTH, None)),
        check_vma=False,
    )
```
